32 devices in a mesh: layers: 2 (over y), row: 4 (over x, core), col: 4 (over z).
Axes of the slice: x: 2, y: 2, z: 4, core: 2. Of those that a mesh axis runs over, the one named last changes fastest.
Arguments:
- factor: bfloat16 [28672, 14336], P(('layers', 'col'), 'row'), parts along dimension 0, may hold values from -1 to 6
- basis_rows: float32 [2048, 14336], P(('layers', 'col'), 'row'), parts along dimension 0, may hold values from -1 to 1
Outputs:
- new_basis: float32 [28672, 1024], P(('layers', 'col'), 'row'), parts along dimension 0
- scales: float32 [2048], P('layers'), parts along dimension 0
The draws below stay inside these ranges and needn't reach their ends.
There are 2 independent parts, one for each index of `layers`. The reference program is written for one: setup_inputs(seed, part) draws one part's arguments, and reference() takes and returns one part's arrays. A program takes and returns all parts, laid end to end along the dimension named above; each array names one. Nothing has to cross between parts.
All inputs are finite; a program needn't handle non-finite values.
Results may differ from the reference program's by a relative error of at most 0.0035.
Values may be sent and summed in bfloat16 or wider, within the bound.
No kernel may reach another device: no remote copies, remote signals or barrier semaphores. Data moves between devices by JAX's collectives and lax.ppermute only.
A program may use at most 256 MiB of HBM per device.

```python
import math
import jax
import jax.numpy as jnp
from jax import lax

ORDER = 14336
BASIS = 1024


def draw_factor(key, part):
    key = jax.random.fold_in(key, 11)
    key_off, key_diag = jax.random.split(key)
    spread = 0.5 / math.sqrt(ORDER)
    off_values = jax.random.normal(key_off, (ORDER, ORDER), jnp.float32) * spread
    diag_values = jnp.exp(jax.random.uniform(key_diag, (ORDER,), jnp.float32, math.log(2.0), math.log(6.0)))
    places = jnp.arange(ORDER)
    on_diag = places[:, None] == places[None, :]
    return jnp.where(on_diag, diag_values[:, None], off_values).astype(jnp.bfloat16)


def draw_basis_rows(key, part):
    key = jax.random.fold_in(key, 23)
    key_noise, key_shared, key_first, key_second = jax.random.split(key, 4)
    width = 1.0 / math.sqrt(ORDER)
    noise = jnp.clip(jax.random.normal(key_noise, (BASIS, ORDER), jnp.float32), -4.0, 4.0)
    shared = jnp.clip(jax.random.normal(key_shared, (2, ORDER), jnp.float32), -4.0, 4.0)
    first = jax.random.uniform(key_first, (BASIS, 1), jnp.float32, 0.2, 0.4)
    second = jax.random.uniform(key_second, (BASIS, 1), jnp.float32, -0.3, 0.3)
    row_scale = jnp.ones((BASIS, 1), jnp.float32)
    values = (noise + first * shared[0][None, :] + second * shared[1][None, :]) * (row_scale * width)
    return jnp.clip(values, -1.0, 1.0)


def setup_inputs(seed: int = 0, part: int = 0) -> dict:
    key_of = jax.random.split(jax.random.key(seed), 3)
    own_keys = jax.random.split(jax.random.fold_in(key_of[2], part), 3)
    return {
        "factor": draw_factor(jax.random.fold_in(jax.random.fold_in(key_of[2], part), 71), part),
        "basis_rows": draw_basis_rows(jax.random.fold_in(jax.random.fold_in(key_of[2], part), 71), part),
    }


def reference(factor, basis_rows):
    rounded = basis_rows.astype(jnp.bfloat16)
    products = jnp.dot(factor.astype(jnp.float32), rounded.T.astype(jnp.float32), preferred_element_type=jnp.float32)
    gram = jnp.dot(products.T.astype(jnp.float32), products.astype(jnp.float32), precision=lax.Precision.HIGHEST, preferred_element_type=jnp.float32)
    lower_factor = jnp.linalg.cholesky(gram)
    solved = jax.scipy.linalg.solve_triangular(lower_factor, products.T, lower=True)
    return (math.sqrt(ORDER) * solved.T, jnp.diagonal(lower_factor))
```

```python
import functools
import math

import jax
import jax.numpy as jnp
from jax import lax
from jax.experimental import pallas as pl
from jax.experimental.pallas import tpu as pltpu
from jax.sharding import PartitionSpec as P

ORDER = 14336
BLOCK = 128
STEP = 8
PANEL = 32
EXACT = lax.Precision.HIGHEST


def dot_rows(x, y):
    return lax.dot_general(x, y, (((0,), (0,)), ((), ())), precision=EXACT, preferred_element_type=jnp.float32)


def dot_plain(x, y):
    return lax.dot_general(x, y, (((1,), (0,)), ((), ())), precision=EXACT, preferred_element_type=jnp.float32)


def factor_block(block):
    pieces = BLOCK // 8
    shape = (8, BLOCK)
    row = lax.broadcasted_iota(jnp.int32, shape, 0)
    column = lax.broadcasted_iota(jnp.int32, shape, 1)
    left = [block[8 * i : 8 * i + 8, :] for i in range(pieces)]
    right = [jnp.where(column == row + 8 * i, 1.0, 0.0).astype(jnp.float32) for i in range(pieces)]
    diagonal = jnp.zeros(shape, jnp.float32)

    def spread(value):
        return jnp.broadcast_to(value, shape)

    for first in range(0, BLOCK, STEP):
        own = first // 8
        end = (first // PANEL + 1) * PANEL // 8
        lanes = [spread(left[own][:, first + s : first + s + 1]) for s in range(STEP)]
        corner = [[spread(lanes[t][s : s + 1, :]) if t >= s else None for t in range(STEP)] for s in range(STEP)]
        rows = [spread(left[own][s : s + 1, :]) for s in range(STEP)]
        sides = [spread(right[own][s : s + 1, :]) for s in range(STEP)]
        columns = [
            {i: spread(left[i][:, first + s : first + s + 1]) for i in range(own + 1, end)} for s in range(STEP)
        ]
        ratio, inverse = {}, []
        for s in range(STEP):
            guess = pl.reciprocal(corner[s][s], approx=True)
            inverse.append(guess * (2.0 - corner[s][s] * guess))
            for t in range(s + 1, STEP):
                ratio[t, s] = corner[s][t] * inverse[s]
                for u in range(t, STEP):
                    corner[t][u] = corner[t][u] - ratio[t, s] * corner[s][u]
        for s in range(STEP):
            for t in range(s + 1, STEP):
                rows[t] = rows[t] - ratio[t, s] * rows[s]
                sides[t] = sides[t] - ratio[t, s] * sides[s]
        if own + 1 < end:
            solved_rows, solved_sides = [None] * STEP, [None] * STEP
            for s in reversed(range(STEP)):
                solved_rows[s] = rows[s] * inverse[s]
                solved_sides[s] = sides[s] * inverse[s]
                for t in range(s + 1, STEP):
                    solved_rows[s] = solved_rows[s] - ratio[t, s] * solved_rows[t]
                    solved_sides[s] = solved_sides[s] - ratio[t, s] * solved_sides[t]
            for i in range(own + 1, end):
                for s in range(STEP):
                    left[i] = left[i] - columns[s][i] * solved_rows[s]
                    right[i] = right[i] - columns[s][i] * solved_sides[s]
        for s in range(STEP):
            root = lax.rsqrt(corner[s][s])
            diagonal = jnp.where(column == first + s, corner[s][s] * root, diagonal)
            left[own] = jnp.where(row == s, rows[s] * root, left[own])
            right[own] = jnp.where(row == s, sides[s] * root, right[own])
        if (first + STEP) % PANEL == 0 and first + STEP < BLOCK:
            start = (first + STEP - PANEL) // 8
            upper = jnp.concatenate(left[start:end], axis=0)
            side = jnp.concatenate(right[start:end], axis=0)
            update = dot_rows(upper, jnp.concatenate([upper, side], axis=1))
            for i in range(end, pieces):
                left[i] = left[i] - update[8 * i : 8 * i + 8, :BLOCK]
                right[i] = right[i] - update[8 * i : 8 * i + 8, BLOCK:]
    return right, diagonal[:1]


def factor_kernel(gram_ref, high_ref, low_ref, scales_ref, work):
    size = gram_ref.shape[0]
    blocks = size // BLOCK
    work[...] = gram_ref[...]
    one = lax.broadcasted_iota(jnp.int32, (BLOCK, BLOCK), 0) == lax.broadcasted_iota(jnp.int32, (BLOCK, BLOCK), 1)

    @pl.loop(0, blocks)
    def _(j):
        own = pl.ds(pl.multiple_of(j * BLOCK, BLOCK), BLOCK)
        pieces, diagonal = factor_block(work[own, own])
        scales_ref[:, own] = diagonal
        work[own, own] = jnp.where(one, 1.0, 0.0).astype(jnp.float32)
        work[own, :] = dot_plain(jnp.concatenate(pieces, axis=0), work[own, :])

        @pl.loop(j + 1, blocks)
        def _(i):
            other = pl.ds(pl.multiple_of(i * BLOCK, BLOCK), BLOCK)
            upper = work[own, other]
            work[other, own] = jnp.zeros((BLOCK, BLOCK), jnp.float32)
            work[other, :] = work[other, :] - dot_rows(upper, work[own, :])

    row = lax.broadcasted_iota(jnp.int32, (size, size), 0)
    column = lax.broadcasted_iota(jnp.int32, (size, size), 1)
    full = jnp.where(column <= row, work[...], 0.0)
    high = full.astype(jnp.bfloat16)
    high_ref[...] = high
    low_ref[...] = (full - high.astype(jnp.float32)).astype(jnp.bfloat16)


def invert_factor(gram):
    size = gram.shape[0]
    vmem = pl.BlockSpec(memory_space=pltpu.VMEM)
    return pl.pallas_call(
        factor_kernel,
        out_shape=[
            jax.ShapeDtypeStruct((size, size), jnp.bfloat16),
            jax.ShapeDtypeStruct((size, size), jnp.bfloat16),
            jax.ShapeDtypeStruct((1, size), jnp.float32),
        ],
        in_specs=[vmem],
        out_specs=[vmem] * 3,
        scratch_shapes=[pltpu.VMEM((size, size), jnp.float32)],
        compiler_params=pltpu.CompilerParams(vmem_limit_bytes=40 * 2**20),
    )(gram)


def local(factor, basis_rows):
    rows, depth = factor.shape
    own_basis = basis_rows.shape[0]
    n_row, n_col = lax.axis_size("row"), lax.axis_size("col")
    basis = own_basis * n_col
    chunks = max(1, min(4, own_basis // 16))
    height = own_basis // chunks
    half = rows // 2
    index = lax.axis_index("row")
    core = index % 2

    def exchange(value, axis, distance):
        size = lax.axis_size(axis)
        return lax.ppermute(value, axis, [(i, i ^ distance) for i in range(size)])

    rounded = basis_rows.astype(jnp.bfloat16)
    parts = []
    for k in range(chunks):
        gathered = lax.all_gather(rounded[k * height : (k + 1) * height], "col", axis=0, tiled=True)
        partial = lax.dot_general(gathered, factor, (((1,), (1,)), ((), ())), preferred_element_type=jnp.float32)
        kept = jnp.where(core == 0, partial[:, :half], partial[:, half:])
        given = jnp.where(core == 0, partial[:, half:], partial[:, :half])
        total = kept + exchange(given, "row", 1)
        distance = 2
        while distance < n_row:
            narrow = total.astype(jnp.bfloat16)
            total = narrow.astype(jnp.float32) + exchange(narrow, "row", distance).astype(jnp.float32)
            distance *= 2
        total = total.astype(jnp.bfloat16)
        other = exchange(total, "row", 1)
        full = jnp.concatenate(
            [jnp.where(core == 0, total, other), jnp.where(core == 0, other, total)], axis=1
        )
        parts.append(full.reshape(n_col, height, rows))
    products = jnp.stack(parts, axis=1).reshape(basis, rows)

    portion = basis // n_row
    own_part = lax.dynamic_slice_in_dim(products, index * portion, portion, 0)
    gram = lax.dot_general(own_part, products, (((1,), (1,)), ((), ())), preferred_element_type=jnp.float32)
    distance = 1
    while distance < n_col:
        gram = gram + exchange(gram, "col", distance)
        distance *= 2
    gram = lax.all_gather(gram, "row", axis=0, tiled=True)
    high, low, scales = invert_factor(gram)
    high = lax.dynamic_slice_in_dim(high, index * portion, portion, 0)
    low = lax.dynamic_slice_in_dim(low, index * portion, portion, 0)
    new_basis = lax.dot_general(
        products, high, (((0,), (1,)), ((), ())), preferred_element_type=jnp.float32
    ) + lax.dot_general(products, low, (((0,), (1,)), ((), ())), preferred_element_type=jnp.float32)
    return (math.sqrt(ORDER) * new_basis, scales[0])


def solution(mesh):
    return jax.shard_map(
        local,
        mesh=mesh,
        in_specs=(P(("layers", "col"), "row"), P(("layers", "col"), "row")),
        out_specs=(P(("layers", "col"), "row"), P("layers")),
        check_vma=False,
    )
```

```python
import functools
import math

import jax
import jax.numpy as jnp
from jax import lax
from jax.experimental import pallas as pl
from jax.experimental.pallas import tpu as pltpu
from jax.sharding import PartitionSpec as P

ORDER = 14336
BLOCK = 128
STEP = 8
PANEL = 32
EXACT = lax.Precision.HIGHEST
COST = 10**10


def dot_rows(x, y):
    return lax.dot_general(x, y, (((0,), (0,)), ((), ())), precision=EXACT, preferred_element_type=jnp.float32)


def dot_plain(x, y):
    return lax.dot_general(x, y, (((1,), (0,)), ((), ())), precision=EXACT, preferred_element_type=jnp.float32)


def factor_block(block):
    pieces = BLOCK // 8
    shape = (8, BLOCK)
    row = lax.broadcasted_iota(jnp.int32, shape, 0)
    column = lax.broadcasted_iota(jnp.int32, shape, 1)
    left = [block[8 * i : 8 * i + 8, :] for i in range(pieces)]
    right = [jnp.where(column == row + 8 * i, 1.0, 0.0).astype(jnp.float32) for i in range(pieces)]

    def spread(value):
        return jnp.broadcast_to(value, shape)

    for first in range(0, BLOCK, STEP):
        own = first // 8
        end = (first // PANEL + 1) * PANEL // 8
        lanes = [spread(left[own][:, first + s : first + s + 1]) for s in range(STEP)]
        corner = [[spread(lanes[t][s : s + 1, :]) if t >= s else None for t in range(STEP)] for s in range(STEP)]
        rows = [spread(left[own][s : s + 1, :]) for s in range(STEP)]
        sides = [spread(right[own][s : s + 1, :]) for s in range(STEP)]
        columns = [
            {i: spread(left[i][:, first + s : first + s + 1]) for i in range(own + 1, end)} for s in range(STEP)
        ]
        ratio, inverse = {}, []
        for s in range(STEP):
            guess = pl.reciprocal(corner[s][s], approx=True)
            inverse.append(guess * (2.0 - corner[s][s] * guess))
            for t in range(s + 1, STEP):
                ratio[t, s] = corner[s][t] * inverse[s]
                for u in range(t, STEP):
                    corner[t][u] = corner[t][u] - ratio[t, s] * corner[s][u]
        for s in range(STEP):
            for t in range(s + 1, STEP):
                rows[t] = rows[t] - ratio[t, s] * rows[s]
                sides[t] = sides[t] - ratio[t, s] * sides[s]
        if own + 1 < end:
            solved_rows, solved_sides = [None] * STEP, [None] * STEP
            for s in reversed(range(STEP)):
                solved_rows[s] = rows[s] * inverse[s]
                solved_sides[s] = sides[s] * inverse[s]
                for t in range(s + 1, STEP):
                    solved_rows[s] = solved_rows[s] - ratio[t, s] * solved_rows[t]
                    solved_sides[s] = solved_sides[s] - ratio[t, s] * solved_sides[t]
            for i in range(own + 1, end):
                for s in range(STEP):
                    left[i] = left[i] - columns[s][i] * solved_rows[s]
                    right[i] = right[i] - columns[s][i] * solved_sides[s]
        for s in range(STEP):
            root = lax.rsqrt(corner[s][s])
            left[own] = jnp.where(row == s, rows[s] * root, left[own])
            right[own] = jnp.where(row == s, sides[s] * root, right[own])
        if (first + STEP) % PANEL == 0 and first + STEP < BLOCK:
            start = (first + STEP - PANEL) // 8
            upper = jnp.concatenate(left[start:end], axis=0)
            side = jnp.concatenate(right[start:end], axis=0)
            update = dot_rows(upper, jnp.concatenate([upper, side], axis=1))
            for i in range(end, pieces):
                left[i] = left[i] - update[8 * i : 8 * i + 8, :BLOCK]
                right[i] = right[i] - update[8 * i : 8 * i + 8, BLOCK:]
    return right


def eliminate(work, first, last):
    blocks = work.shape[0] // BLOCK
    one = lax.broadcasted_iota(jnp.int32, (BLOCK, BLOCK), 0) == lax.broadcasted_iota(jnp.int32, (BLOCK, BLOCK), 1)

    @pl.loop(first, last)
    def _(j):
        own = pl.ds(pl.multiple_of(j * BLOCK, BLOCK), BLOCK)
        pieces = factor_block(work[own, own])
        work[own, own] = jnp.where(one, 1.0, 0.0).astype(jnp.float32)
        work[own, :] = dot_plain(jnp.concatenate(pieces, axis=0), work[own, :])

        @pl.loop(j + 1, blocks)
        def _(i):
            other = pl.ds(pl.multiple_of(i * BLOCK, BLOCK), BLOCK)
            upper = work[own, other]
            work[other, own] = jnp.zeros((BLOCK, BLOCK), jnp.float32)
            work[other, :] = work[other, :] - dot_rows(upper, work[own, :])


def lower_part(value):
    row = lax.broadcasted_iota(jnp.int32, value.shape, 0)
    return jnp.where(lax.broadcasted_iota(jnp.int32, value.shape, 1) <= row, value, 0.0)


def pairs_of(n):
    return [(0, False)] + [(d, 2 * d == n) for d in range(1, n // 2 + 1)]


def own_pair(r, offset, n):
    if 2 * offset == n:
        low = r % offset
        return low, low + offset
    other = (r + offset) % n
    return jnp.minimum(r, other), jnp.maximum(r, other)


def place_symmetric(matrix, held, n, block):
    for r in range(n):
        row = 0
        for offset, split in pairs_of(n):
            if split:
                i, j = r % offset, r % offset + offset
                height, start = block // 2, r // offset * (block // 2)
            else:
                i, j = min(r, (r + offset) % n), max(r, (r + offset) % n)
                height, start = block, 0
            matrix[i * block + start : i * block + start + height, j * block : (j + 1) * block] = held(
                r, row, height
            )
            row += height
    return row


def first_kernel(n, order, steps, r_ref, *refs):
    held, work, stack = refs[:n], refs[n], refs[n + 1]
    size = work.shape[0]
    r = r_ref[0]
    for value, distance in zip(held, order):
        stack[r ^ distance] = value[...]
    work[...] = jnp.zeros_like(work)
    place_symmetric(work, lambda d, row, height: stack[d, row : row + height, :], n, size // n)
    eliminate(work, 0, steps)


def second_kernel(steps, before_ref, work):
    work[...] = before_ref[...]
    eliminate(work, steps, work.shape[0] // BLOCK)


def last_kernel(n, order, r_ref, *refs):
    held, left_ref = refs[:n], refs[n]
    high_ref, low_ref, scales_ref, stack, whole, cross, work = refs[n + 1 :]
    size = left_ref.shape[0]
    block = size // n
    r = r_ref[0]
    for value, distance in zip(held, order):
        stack[r ^ distance] = value[...]
    corner = place_symmetric(work, lambda d, row, height: stack[d, row : row + height, :], n, block)
    for d in range(n):
        for j in range(n):
            cross[d * block : (d + 1) * block, j * block : (j + 1) * block] = stack[
                d, corner + j * block : corner + (j + 1) * block, :
            ]
    inverse = lower_part(left_ref[...])
    whole[:size, :size] = inverse
    whole[:size, size:] = jnp.zeros((size, size), jnp.float32)
    cross[...] = dot_plain(inverse, cross[...])
    row = lax.broadcasted_iota(jnp.int32, (size, size), 0)
    column = lax.broadcasted_iota(jnp.int32, (size, size), 1)
    upper = jnp.where(row // block <= column // block, work[...], 0.0)
    work[...] = upper - dot_rows(cross[...], cross[...])
    eliminate(work, 0, size // BLOCK)
    inverse = lower_part(work[...])
    whole[size:, size:] = inverse
    whole[size:, :size] = -dot_plain(inverse, dot_rows(cross[...], whole[:size, :size]))
    one = lax.broadcasted_iota(jnp.int32, (BLOCK, BLOCK), 0) == lax.broadcasted_iota(jnp.int32, (BLOCK, BLOCK), 1)
    for first in range(0, 2 * size, BLOCK):
        at = slice(first, first + BLOCK)
        scales_ref[:, at] = 1.0 / jnp.sum(jnp.where(one, whole[at, at], 0.0), axis=0, keepdims=True)
    portion = high_ref.shape[0]
    rows = whole[pl.ds(pl.multiple_of(r * portion, portion), portion), :]
    high = rows.astype(jnp.bfloat16)
    high_ref[...] = high
    low_ref[...] = (rows - high.astype(jnp.float32)).astype(jnp.bfloat16)


VMEM = pl.BlockSpec(memory_space=pltpu.VMEM)
SMEM = pl.BlockSpec(memory_space=pltpu.SMEM)


def kernel_options():
    return {
        "compiler_params": pltpu.CompilerParams(vmem_limit_bytes=40 * 2**20),
        "cost_estimate": pl.CostEstimate(flops=COST, bytes_accessed=0, transcendentals=0),
    }


def invert_factor(index, order, corner, rest, size):
    n = len(order)
    half = size // 2
    square = jax.ShapeDtypeStruct((half, half), jnp.float32)
    steps = half // BLOCK // 2
    work = pl.pallas_call(
        functools.partial(first_kernel, n, order, steps),
        out_shape=square,
        in_specs=[SMEM] + [VMEM] * n,
        out_specs=VMEM,
        scratch_shapes=[pltpu.VMEM((n,) + corner[0].shape, jnp.float32)],
        **kernel_options(),
    )(index, *corner)
    work = pl.pallas_call(
        functools.partial(second_kernel, steps),
        out_shape=square,
        in_specs=[VMEM],
        out_specs=VMEM,
        **kernel_options(),
    )(work)
    portion = size // n
    return pl.pallas_call(
        functools.partial(last_kernel, n, order),
        out_shape=[
            jax.ShapeDtypeStruct((portion, size), jnp.bfloat16),
            jax.ShapeDtypeStruct((portion, size), jnp.bfloat16),
            jax.ShapeDtypeStruct((1, size), jnp.float32),
        ],
        in_specs=[SMEM] + [VMEM] * (n + 1),
        out_specs=[VMEM] * 3,
        scratch_shapes=[
            pltpu.VMEM((n,) + rest[0].shape, jnp.float32),
            pltpu.VMEM((size, size), jnp.float32),
            pltpu.VMEM((half, half), jnp.float32),
            pltpu.VMEM((half, half), jnp.float32),
        ],
        **kernel_options(),
    )(index, *rest, work)


def multiply_kernel(layout, tile, which_ref, *refs):
    candidates, factor_ref, out_ref = refs[:-6], refs[-6], refs[-5]
    block, weights, block_ready, ready = refs[-4:]
    half = out_ref.shape[2]
    tiles = half // tile
    core = which_ref[0]
    places = []
    for i in range(2 * tiles):
        part = lax.rem(i // tiles + core + 1, 2)
        places.append(pl.ds(pl.multiple_of(part * half + i % tiles * tile, tile), tile))
    first, row = 0, 0
    for piece, count in enumerate(layout):
        height = candidates[first].shape[0]
        for k in range(count):

            @pl.when(which_ref[piece + 1] == k)
            def _(k=k, first=first, row=row, height=height, piece=piece):
                pltpu.make_async_copy(
                    candidates[first + k], block.at[pl.ds(row, height)], block_ready.at[piece]
                ).start()

        first, row = first + count, row + height
    copies = [pltpu.make_async_copy(factor_ref.at[p], weights.at[i], ready.at[i]) for i, p in enumerate(places)]
    for copy in copies:
        copy.start()
    first, row = 0, 0
    for piece, count in enumerate(layout):
        height = candidates[first].shape[0]
        pltpu.make_async_copy(candidates[first], block.at[pl.ds(row, height)], block_ready.at[piece]).wait()
        first, row = first + count, row + height
    for i, copy in enumerate(copies):
        copy.wait()
        out_ref[i // tiles, :, i % tiles * tile : (i % tiles + 1) * tile] = lax.dot_general(
            block[...], weights[i], (((1,), (1,)), ((), ())), preferred_element_type=jnp.float32
        )


def multiply(which, pieces, factor):
    rows, depth = factor.shape
    columns = sum(candidates[0].shape[0] for candidates in pieces)
    half = rows // 2
    tile = next((t for t in (896, 512, 256) if half % t == 0), half)
    tiles = 2 * half // tile
    layout = tuple(len(candidates) for candidates in pieces)
    return pl.pallas_call(
        functools.partial(multiply_kernel, layout, tile),
        in_specs=[pl.BlockSpec(memory_space=pltpu.SMEM)] + [pl.BlockSpec(memory_space=pl.ANY)] * (sum(layout) + 1),
        out_specs=pl.BlockSpec(memory_space=pltpu.VMEM),
        scratch_shapes=[
            pltpu.VMEM((columns, depth), jnp.bfloat16),
            pltpu.VMEM((tiles, tile, depth), jnp.bfloat16),
            pltpu.SemaphoreType.DMA((len(layout),)),
            pltpu.SemaphoreType.DMA((tiles,)),
        ],
        out_shape=jax.ShapeDtypeStruct((2, columns, half), jnp.float32),
        compiler_params=pltpu.CompilerParams(vmem_limit_bytes=40 * 2**20),
        cost_estimate=pl.CostEstimate(flops=COST, bytes_accessed=0, transcendentals=0),
    )(which, *[c for candidates in pieces for c in candidates], factor)


def local(factor, basis_rows):
    rows, depth = factor.shape
    own_basis = basis_rows.shape[0]
    n_row, n_col = lax.axis_size("row"), lax.axis_size("col")
    basis = own_basis * n_col
    half = rows // 2
    index = lax.axis_index("row")
    plane = lax.axis_index("col")
    core = index % 2

    def exchange(value, axis, distance):
        size = lax.axis_size(axis)
        return lax.ppermute(value, axis, [(i, i ^ distance) for i in range(size)])

    rounded = basis_rows.astype(jnp.bfloat16)
    cut = own_basis // 2

    def stream(part):
        below, above = [part], [part]
        for hop in range(1, n_col):
            below.append(lax.ppermute(below[-1], "col", [(i, i + 1) for i in range(hop - 1, n_col - 1)]))
            above.append(lax.ppermute(above[-1], "col", [(i + 1, i) for i in range(0, n_col - hop)]))
        return below, above

    halves = [jnp.zeros((basis, half), jnp.bfloat16)] * 2

    def add_unit(halves, pieces):
        blocks = [jnp.where(hop <= plane, plane - hop, hop) for hop, _, _ in pieces]
        which = jnp.stack([core] + [jnp.where(hop <= plane, 0, hop - plane) for hop, _, _ in pieces])
        products = multiply(which.astype(jnp.int32), [candidates for _, _, candidates in pieces], factor)
        total = products[1] + exchange(products[0], "row", 1)
        distance = 2
        while distance < n_row:
            narrow = total.astype(jnp.bfloat16)
            total = narrow.astype(jnp.float32) + exchange(narrow, "row", distance).astype(jnp.float32)
            distance *= 2
        total = total.astype(jnp.bfloat16)
        other = exchange(total, "row", 1)
        row = 0
        for (_, offset, candidates), block in zip(pieces, blocks):
            height = candidates[0].shape[0]
            start = block * own_basis + offset
            halves = [
                lax.dynamic_update_slice_in_dim(h, v[row : row + height], start, 0)
                for h, v in zip(halves, (total, other))
            ]
            row += height
        return halves

    halves = add_unit(halves, [(0, 0, [rounded])])
    streams = []
    for offset, part in ((0, rounded[:cut]), (cut, rounded[cut:])):
        below, above = stream(part)
        streams.append([(hop, offset, [below[hop]] + above[1 : hop + 1]) for hop in range(1, n_col)])
    units = [list(pair) for pair in zip(*streams)]
    units = units[:-1] + [[piece] for piece in units[-1]]
    for unit in units:
        halves = add_unit(halves, unit)

    side = basis // 2
    block = side // n_row

    def gram(rows, columns):
        return sum(
            lax.dot_general(
                lax.dynamic_slice_in_dim(h, rows[0], rows[1], 0),
                lax.dynamic_slice_in_dim(h, columns[0], columns[1], 0),
                (((1,), (1,)), ((), ())),
                preferred_element_type=jnp.float32,
            )
            for h in halves
        )

    def share(start):
        found = []
        for offset, split in pairs_of(n_row):
            i, j = own_pair(index, offset, n_row) if offset else (index, index)
            height = block // 2 if split else block
            first = start + i * block + (index // offset * height if split else 0)
            found.append(gram((first, height), (start + j * block, block)))
        return found

    corner = jnp.concatenate(share(0), axis=0)
    cross = gram((index * block, block), (side, side))
    rest = jnp.concatenate(share(side) + [cross[:, j * block : (j + 1) * block] for j in range(n_row)], axis=0)

    def over_planes(value):
        if n_col == 4:
            toward = lax.ppermute(value, "col", [(0, 1), (3, 2)])
            value = value + toward
            value = value + lax.ppermute(value, "col", [(1, 2), (2, 1)])
            outward = lax.ppermute(value, "col", [(1, 0), (2, 3)])
            return jnp.where((plane == 0) | (plane == 3), outward, value)
        distance = 1
        while distance < n_col:
            value = value + exchange(value, "col", distance)
            distance *= 2
        return value

    def over_row(value):
        held = {0: value}
        distances = [1 << k for k in range(1, n_row.bit_length() - 1)] + [1]
        for distance in distances:
            held |= {d ^ distance: exchange(v, "row", distance) for d, v in held.items()}
        return held

    corner, rest = over_row(over_planes(corner)), over_row(over_planes(rest))
    order = tuple(corner)
    high, low, scales = invert_factor(
        index.reshape(1).astype(jnp.int32), order, list(corner.values()), list(rest.values()), basis
    )
    first = jnp.where(core == 0, halves[0], halves[1])
    second = jnp.where(core == 0, halves[1], halves[0])
    products = jnp.concatenate([first, second], axis=1)
    new_basis = lax.dot_general(
        products, high, (((0,), (1,)), ((), ())), preferred_element_type=jnp.float32
    ) + lax.dot_general(products, low, (((0,), (1,)), ((), ())), preferred_element_type=jnp.float32)
    return (math.sqrt(ORDER) * new_basis, scales[0])


def solution(mesh):
    return jax.shard_map(
        local,
        mesh=mesh,
        in_specs=(P(("layers", "col"), "row"), P(("layers", "col"), "row")),
        out_specs=(P(("layers", "col"), "row"), P("layers")),
        check_vma=False,
    )
```

```python
import functools
import math

import jax
import jax.numpy as jnp
from jax import lax
from jax.experimental import pallas as pl
from jax.experimental.pallas import tpu as pltpu
from jax.sharding import PartitionSpec as P

ORDER = 14336
BLOCK = 128
STEP = 8
PANEL = 32
EXACT = lax.Precision.HIGHEST
COST = 10**10


def dot_exact(x, y):
    return lax.dot_general(x, y, (((0,), (0,)), ((), ())), precision=EXACT, preferred_element_type=jnp.float32)


def split(x):
    high = x.astype(jnp.bfloat16)
    return high, (x - high.astype(jnp.float32)).astype(jnp.bfloat16)


def dot_split(x, y, dimension):
    (x, x_low), (y, y_low) = split(x), split(y)

    def dot(u, v):
        return lax.dot_general(u, v, (((dimension,), (0,)), ((), ())), preferred_element_type=jnp.float32)

    return dot(x, y) + (dot(x_low, y) + dot(x, y_low))


def dot_rows(x, y):
    return dot_split(x, y, 0)


def dot_plain(x, y):
    return dot_split(x, y, 1)


def tree(terms):
    while len(terms) > 1:
        terms = [a + b for a, b in zip(terms[::2], terms[1::2])]
    return terms[0]


def factor_block(block):
    pieces = BLOCK // 8
    shape = (8, BLOCK)
    row = lax.broadcasted_iota(jnp.int32, shape, 0)
    column = lax.broadcasted_iota(jnp.int32, shape, 1)
    left = [block[8 * i : 8 * i + 8, :] for i in range(pieces)]
    right = [jnp.where(column == row + 8 * i, 1.0, 0.0).astype(jnp.float32) for i in range(pieces)]

    def spread(value):
        return jnp.broadcast_to(value, shape)

    for first in range(0, BLOCK, STEP):
        own = first // 8
        end = (first // PANEL + 1) * PANEL // 8
        lanes = [spread(left[own][:, first + s : first + s + 1]) for s in range(STEP)]
        corner = [[spread(lanes[t][s : s + 1, :]) if t >= s else None for t in range(STEP)] for s in range(STEP)]
        rows = [spread(left[own][s : s + 1, :]) for s in range(STEP)]
        sides = [spread(right[own][s : s + 1, :]) for s in range(STEP)]
        columns = [
            {i: spread(left[i][:, first + s : first + s + 1]) for i in range(own + 1, end)} for s in range(STEP)
        ]
        ratio, inverse, roots = {}, [], []
        for s in range(STEP):
            roots.append(lax.rsqrt(corner[s][s]))
            scaled = [None if u <= s else corner[s][u] * roots[s] for u in range(STEP)]
            inverse.append(roots[s] * roots[s])
            for t in range(s + 1, STEP):
                ratio[t, s] = scaled[t] * roots[s]
                for u in range(t, STEP):
                    corner[t][u] = corner[t][u] - scaled[t] * scaled[u]
        for s in range(STEP):
            for t in range(s + 1, STEP):
                rows[t] = rows[t] - ratio[t, s] * rows[s]
                sides[t] = sides[t] - ratio[t, s] * sides[s]
        if own + 1 < end:
            solved_rows, solved_sides = [None] * STEP, [None] * STEP
            for s in reversed(range(STEP)):
                solved_rows[s] = rows[s] * inverse[s]
                solved_sides[s] = sides[s] * inverse[s]
                for t in range(s + 1, STEP):
                    solved_rows[s] = solved_rows[s] - ratio[t, s] * solved_rows[t]
                    solved_sides[s] = solved_sides[s] - ratio[t, s] * solved_sides[t]
            for i in range(own + 1, end):
                left[i] = left[i] - tree([columns[s][i] * solved_rows[s] for s in range(STEP)])
                right[i] = right[i] - tree([columns[s][i] * solved_sides[s] for s in range(STEP)])
        for s in range(STEP):
            root = roots[s]
            left[own] = jnp.where(row == s, rows[s] * root, left[own])
            right[own] = jnp.where(row == s, sides[s] * root, right[own])
        if (first + STEP) % PANEL == 0 and first + STEP < BLOCK:
            start = (first + STEP - PANEL) // 8
            upper = jnp.concatenate(left[start:end], axis=0)
            side = jnp.concatenate(right[start:end], axis=0)
            update = dot_exact(upper, jnp.concatenate([upper, side], axis=1))
            for i in range(end, pieces):
                left[i] = left[i] - update[8 * i : 8 * i + 8, :BLOCK]
                right[i] = right[i] - update[8 * i : 8 * i + 8, BLOCK:]
    return right


def eliminate(work, first, last):
    blocks = work.shape[0] // BLOCK
    one = lax.broadcasted_iota(jnp.int32, (BLOCK, BLOCK), 0) == lax.broadcasted_iota(jnp.int32, (BLOCK, BLOCK), 1)

    @pl.loop(first, last)
    def _(j):
        own = pl.ds(pl.multiple_of(j * BLOCK, BLOCK), BLOCK)
        pieces = factor_block(work[own, own])
        work[own, own] = jnp.where(one, 1.0, 0.0).astype(jnp.float32)
        work[own, :] = dot_plain(jnp.concatenate(pieces, axis=0), work[own, :])

        @pl.loop(j + 1, blocks)
        def _(i):
            other = pl.ds(pl.multiple_of(i * BLOCK, BLOCK), BLOCK)
            upper = work[own, other]
            work[other, own] = jnp.zeros((BLOCK, BLOCK), jnp.float32)
            work[other, :] = work[other, :] - dot_rows(upper, work[own, :])


def lower_part(value):
    row = lax.broadcasted_iota(jnp.int32, value.shape, 0)
    return jnp.where(lax.broadcasted_iota(jnp.int32, value.shape, 1) <= row, value, 0.0)


def pairs_of(n):
    return [(0, False)] + [(d, 2 * d == n) for d in range(1, n // 2 + 1)]


def own_pair(r, offset, n):
    if 2 * offset == n:
        low = r % offset
        return low, low + offset
    other = (r + offset) % n
    return jnp.minimum(r, other), jnp.maximum(r, other)


def place_symmetric(matrix, held, n, block):
    for r in range(n):
        row = 0
        for offset, split in pairs_of(n):
            if split:
                i, j = r % offset, r % offset + offset
                height, start = block // 2, r // offset * (block // 2)
            else:
                i, j = min(r, (r + offset) % n), max(r, (r + offset) % n)
                height, start = block, 0
            matrix[i * block + start : i * block + start + height, j * block : (j + 1) * block] = held(
                r, row, height
            )
            row += height
    return row


def first_kernel(n, order, steps, r_ref, *refs):
    held, work, stack = refs[:n], refs[n], refs[n + 1]
    size = work.shape[0]
    r = r_ref[0]
    for value, distance in zip(held, order):
        stack[r ^ distance] = value[...]
    work[...] = jnp.zeros_like(work)
    place_symmetric(work, lambda d, row, height: stack[d, row : row + height, :], n, size // n)
    eliminate(work, 0, steps)


def second_kernel(steps, before_ref, work):
    work[...] = before_ref[...]
    eliminate(work, steps, work.shape[0] // BLOCK)


def last_kernel(n, order, r_ref, *refs):
    held, left_ref = refs[:n], refs[n]
    high_ref, low_ref, scales_ref, stack, whole, cross, work = refs[n + 1 :]
    size = left_ref.shape[0]
    block = size // n
    r = r_ref[0]
    for value, distance in zip(held, order):
        stack[r ^ distance] = value[...]
    corner = place_symmetric(work, lambda d, row, height: stack[d, row : row + height, :], n, block)
    for d in range(n):
        for j in range(n):
            cross[d * block : (d + 1) * block, j * block : (j + 1) * block] = stack[
                d, corner + j * block : corner + (j + 1) * block, :
            ]
    inverse = lower_part(left_ref[...])
    whole[:size, :size] = inverse
    whole[:size, size:] = jnp.zeros((size, size), jnp.float32)
    cross[...] = dot_plain(inverse, cross[...])
    row = lax.broadcasted_iota(jnp.int32, (size, size), 0)
    column = lax.broadcasted_iota(jnp.int32, (size, size), 1)
    upper = jnp.where(row // block <= column // block, work[...], 0.0)
    work[...] = upper - dot_rows(cross[...], cross[...])
    eliminate(work, 0, size // BLOCK)
    inverse = lower_part(work[...])
    whole[size:, size:] = inverse
    whole[size:, :size] = -dot_plain(inverse, dot_rows(cross[...], whole[:size, :size]))
    one = lax.broadcasted_iota(jnp.int32, (BLOCK, BLOCK), 0) == lax.broadcasted_iota(jnp.int32, (BLOCK, BLOCK), 1)
    for first in range(0, 2 * size, BLOCK):
        at = slice(first, first + BLOCK)
        scales_ref[:, at] = 1.0 / jnp.sum(jnp.where(one, whole[at, at], 0.0), axis=0, keepdims=True)
    portion = high_ref.shape[0]
    rows = whole[pl.ds(pl.multiple_of(r * portion, portion), portion), :]
    high = rows.astype(jnp.bfloat16)
    high_ref[...] = high
    low_ref[...] = (rows - high.astype(jnp.float32)).astype(jnp.bfloat16)


VMEM = pl.BlockSpec(memory_space=pltpu.VMEM)
SMEM = pl.BlockSpec(memory_space=pltpu.SMEM)


def kernel_options():
    return {
        "compiler_params": pltpu.CompilerParams(vmem_limit_bytes=40 * 2**20),
        "cost_estimate": pl.CostEstimate(flops=COST, bytes_accessed=0, transcendentals=0),
    }


def begin_factor(index, order, corner, half):
    n = len(order)
    return pl.pallas_call(
        functools.partial(first_kernel, n, order, half // BLOCK // 2),
        out_shape=jax.ShapeDtypeStruct((half, half), jnp.float32),
        in_specs=[SMEM] + [VMEM] * n,
        out_specs=VMEM,
        scratch_shapes=[pltpu.VMEM((n,) + corner[0].shape, jnp.float32)],
        **kernel_options(),
    )(index, *corner)


def go_on_factor(work):
    return pl.pallas_call(
        functools.partial(second_kernel, work.shape[0] // BLOCK // 2),
        out_shape=jax.ShapeDtypeStruct(work.shape, jnp.float32),
        in_specs=[VMEM],
        out_specs=VMEM,
        **kernel_options(),
    )(work)


def end_factor(index, order, rest, work, size):
    n = len(order)
    half = size // 2
    portion = size // n
    return pl.pallas_call(
        functools.partial(last_kernel, n, order),
        out_shape=[
            jax.ShapeDtypeStruct((portion, size), jnp.bfloat16),
            jax.ShapeDtypeStruct((portion, size), jnp.bfloat16),
            jax.ShapeDtypeStruct((1, size), jnp.float32),
        ],
        in_specs=[SMEM] + [VMEM] * (n + 1),
        out_specs=[VMEM] * 3,
        scratch_shapes=[
            pltpu.VMEM((n,) + rest[0].shape, jnp.float32),
            pltpu.VMEM((size, size), jnp.float32),
            pltpu.VMEM((half, half), jnp.float32),
            pltpu.VMEM((half, half), jnp.float32),
        ],
        **kernel_options(),
    )(index, *rest, work)


def multiply_kernel(layout, tile, which_ref, *refs):
    candidates, factor_ref, out_ref = refs[:-6], refs[-6], refs[-5]
    block, weights, block_ready, ready = refs[-4:]
    half = out_ref.shape[2]
    tiles = half // tile
    core = which_ref[0]
    places = []
    for i in range(2 * tiles):
        part = lax.rem(i // tiles + core + 1, 2)
        places.append(pl.ds(pl.multiple_of(part * half + i % tiles * tile, tile), tile))
    first, row = 0, 0
    for piece, count in enumerate(layout):
        height = candidates[first].shape[0]
        for k in range(count):

            @pl.when(which_ref[piece + 1] == k)
            def _(k=k, first=first, row=row, height=height, piece=piece):
                pltpu.make_async_copy(
                    candidates[first + k], block.at[pl.ds(row, height)], block_ready.at[piece]
                ).start()

        first, row = first + count, row + height
    copies = [pltpu.make_async_copy(factor_ref.at[p], weights.at[i], ready.at[i]) for i, p in enumerate(places)]
    for copy in copies:
        copy.start()
    first, row = 0, 0
    for piece, count in enumerate(layout):
        height = candidates[first].shape[0]
        pltpu.make_async_copy(candidates[first], block.at[pl.ds(row, height)], block_ready.at[piece]).wait()
        first, row = first + count, row + height
    for i, copy in enumerate(copies):
        copy.wait()
        out_ref[i // tiles, :, i % tiles * tile : (i % tiles + 1) * tile] = lax.dot_general(
            block[...], weights[i], (((1,), (1,)), ((), ())), preferred_element_type=jnp.float32
        )


def multiply(which, pieces, factor):
    rows, depth = factor.shape
    columns = sum(candidates[0].shape[0] for candidates in pieces)
    half = rows // 2
    tile = next((t for t in (896, 512, 256) if half % t == 0), half)
    tiles = 2 * half // tile
    layout = tuple(len(candidates) for candidates in pieces)
    return pl.pallas_call(
        functools.partial(multiply_kernel, layout, tile),
        in_specs=[pl.BlockSpec(memory_space=pltpu.SMEM)] + [pl.BlockSpec(memory_space=pl.ANY)] * (sum(layout) + 1),
        out_specs=pl.BlockSpec(memory_space=pltpu.VMEM),
        scratch_shapes=[
            pltpu.VMEM((columns, depth), jnp.bfloat16),
            pltpu.VMEM((tiles, tile, depth), jnp.bfloat16),
            pltpu.SemaphoreType.DMA((len(layout),)),
            pltpu.SemaphoreType.DMA((tiles,)),
        ],
        out_shape=jax.ShapeDtypeStruct((2, columns, half), jnp.float32),
        compiler_params=pltpu.CompilerParams(vmem_limit_bytes=40 * 2**20),
        cost_estimate=pl.CostEstimate(flops=COST, bytes_accessed=0, transcendentals=0),
    )(which, *[c for candidates in pieces for c in candidates], factor)


def local(factor, basis_rows):
    rows, depth = factor.shape
    own_basis = basis_rows.shape[0]
    n_row, n_col = lax.axis_size("row"), lax.axis_size("col")
    basis = own_basis * n_col
    half = rows // 2
    index = lax.axis_index("row")
    plane = lax.axis_index("col")
    core = index % 2

    def exchange(value, axis, distance):
        size = lax.axis_size(axis)
        return lax.ppermute(value, axis, [(i, i ^ distance) for i in range(size)])

    rounded = basis_rows.astype(jnp.bfloat16)
    cut = own_basis // 2

    def stream(part):
        below, above = [part], [part]
        for hop in range(1, n_col):
            below.append(lax.ppermute(below[-1], "col", [(i, i + 1) for i in range(hop - 1, n_col - 1)]))
            above.append(lax.ppermute(above[-1], "col", [(i + 1, i) for i in range(0, n_col - hop)]))
        return below, above

    halves = [jnp.zeros((basis, half), jnp.bfloat16)] * 2

    def after(value, *others):
        return lax.optimization_barrier((value, others))[0]

    def begin_unit(pieces, *others):
        which = jnp.stack([core] + [jnp.where(hop <= plane, 0, hop - plane) for hop, _, _ in pieces])
        which = after(which.astype(jnp.int32), *others)
        products = multiply(which, [candidates for _, _, candidates in pieces], factor)
        return products[1] + exchange(products[0], "row", 1)

    def sum_chips(total):
        distance = 2
        while distance < n_row:
            narrow = total.astype(jnp.bfloat16)
            total = narrow.astype(jnp.float32) + exchange(narrow, "row", distance).astype(jnp.float32)
            distance *= 2
        return total.astype(jnp.bfloat16)

    def end_unit(halves, pieces, total):
        other = exchange(total, "row", 1)
        row = 0
        for hop, offset, candidates in pieces:
            height = candidates[0].shape[0]
            start = jnp.where(hop <= plane, plane - hop, hop) * own_basis + offset
            halves = [
                lax.dynamic_update_slice_in_dim(h, v[row : row + height], start, 0)
                for h, v in zip(halves, (total, other))
            ]
            row += height
        return halves

    streams = []
    for offset, part in ((0, rounded[:cut]), (cut, rounded[cut:])):
        below, above = stream(part)
        streams.append([(hop, offset, [below[hop]] + above[1 : hop + 1]) for hop in range(1, n_col)])
    units = [[(0, 0, [rounded])]] + [list(pair) for pair in zip(*streams)]
    units = units[:-1] + [[piece] for piece in units[-1]]
    begun, sums = [], []
    for k, unit in enumerate(units):
        first = [begun[j] for i, j in [(4, 2)] if i == k] + [sums[j] for i, j in [(4, 1)] if i == k]
        begun.append(begin_unit(unit, *first))
        sums.append(sum_chips(begun[-1]))
    for unit, total in zip(units, sums):
        halves = end_unit(halves, unit, total)

    side = basis // 2
    block = side // n_row

    def gram(rows, columns):
        return sum(
            lax.dot_general(
                lax.dynamic_slice_in_dim(h, rows[0], rows[1], 0),
                lax.dynamic_slice_in_dim(h, columns[0], columns[1], 0),
                (((1,), (1,)), ((), ())),
                preferred_element_type=jnp.float32,
            )
            for h in halves
        )

    def share(start):
        found = []
        for offset, split in pairs_of(n_row):
            i, j = own_pair(index, offset, n_row) if offset else (index, index)
            height = block // 2 if split else block
            first = start + i * block + (index // offset * height if split else 0)
            found.append(gram((first, height), (start + j * block, block)))
        return found

    corner = jnp.concatenate(share(0), axis=0)
    cross = gram((index * block, block), (side, side))
    rest = jnp.concatenate(share(side) + [cross[:, j * block : (j + 1) * block] for j in range(n_row)], axis=0)

    def over_planes(value, others):
        if n_col == 4:
            toward = value + lax.ppermute(value, "col", [(0, 1), (3, 2)])
            if others is not None:
                toward = after(toward, others)
            both = toward + lax.ppermute(toward, "col", [(1, 2), (2, 1)])
            outward = lax.ppermute(both, "col", [(1, 0), (2, 3)])
            total = jnp.where((plane == 0) | (plane == 3), outward, both)
            return total, total
        distance = 1
        while distance < n_col:
            value = value + exchange(value, "col", distance)
            distance *= 2
        return value, value

    def over_row(value, *others):
        held = {0: value}
        distances = [1 << k for k in range(1, n_row.bit_length() - 1)] + [1]
        for distance in distances:
            if distance == 1 and others:
                held = {d: after(v, *others) for d, v in held.items()}
            held |= {d ^ distance: exchange(v, "row", distance) for d, v in held.items()}
        return held

    corner, passed = over_planes(corner, None)
    rest, _ = over_planes(rest, passed)
    corner = over_row(corner)
    order = tuple(corner)
    device = index.reshape(1).astype(jnp.int32)
    work = begin_factor(device, order, list(corner.values()), side)
    rest = after(rest, work)
    work = go_on_factor(work)
    rest = over_row(rest, work)
    high, low, scales = end_factor(device, order, list(rest.values()), work, basis)
    first = jnp.where(core == 0, halves[0], halves[1])
    second = jnp.where(core == 0, halves[1], halves[0])
    products = jnp.concatenate([first, second], axis=1)
    new_basis = lax.dot_general(
        products, high, (((0,), (1,)), ((), ())), preferred_element_type=jnp.float32
    ) + lax.dot_general(products, low, (((0,), (1,)), ((), ())), preferred_element_type=jnp.float32)
    return (math.sqrt(ORDER) * new_basis, scales[0])


def solution(mesh):
    return jax.shard_map(
        local,
        mesh=mesh,
        in_specs=(P(("layers", "col"), "row"), P(("layers", "col"), "row")),
        out_specs=(P(("layers", "col"), "row"), P("layers")),
        check_vma=False,
    )
```

```python
import functools
import math

import jax
import jax.numpy as jnp
from jax import lax
from jax.experimental import pallas as pl
from jax.experimental.pallas import tpu as pltpu
from jax.sharding import PartitionSpec as P

ORDER = 14336
BLOCK = 128
STEP = 8
PANEL = 64
EXACT = lax.Precision.HIGHEST
COST = 10**10


def dot_exact(x, y):
    return lax.dot_general(x, y, (((0,), (0,)), ((), ())), precision=EXACT, preferred_element_type=jnp.float32)


def split(x):
    high = x.astype(jnp.bfloat16)
    return high, (x - high.astype(jnp.float32)).astype(jnp.bfloat16)


def dot_split(x, y, dimension):
    (x, x_low), (y, y_low) = split(x), split(y)

    def dot(u, v):
        return lax.dot_general(u, v, (((dimension,), (0,)), ((), ())), preferred_element_type=jnp.float32)

    return dot(x, y) + (dot(x_low, y) + dot(x, y_low))


def dot_rows(x, y):
    return dot_split(x, y, 0)


def dot_plain(x, y):
    return dot_split(x, y, 1)


def tree(terms):
    while len(terms) > 1:
        terms = [a + b for a, b in zip(terms[::2], terms[1::2])]
    return terms[0]


def factor_block(block):
    pieces = BLOCK // 8
    shape = (8, BLOCK)
    row = lax.broadcasted_iota(jnp.int32, shape, 0)
    column = lax.broadcasted_iota(jnp.int32, shape, 1)
    left = [block[8 * i : 8 * i + 8, :] for i in range(pieces)]
    right = [jnp.where(column == row + 8 * i, 1.0, 0.0).astype(jnp.float32) for i in range(pieces)]

    def spread(value):
        return jnp.broadcast_to(value, shape)

    for first in range(0, BLOCK, STEP):
        own = first // 8
        end = (first // PANEL + 1) * PANEL // 8
        lanes = [spread(left[own][:, first + s : first + s + 1]) for s in range(STEP)]
        corner = [[spread(lanes[t][s : s + 1, :]) if t >= s else None for t in range(STEP)] for s in range(STEP)]
        rows = [spread(left[own][s : s + 1, :]) for s in range(STEP)]
        sides = [spread(right[own][s : s + 1, :]) for s in range(STEP)]
        columns = [
            {i: spread(left[i][:, first + s : first + s + 1]) for i in range(own + 1, end)} for s in range(STEP)
        ]
        ratio, inverse, roots = {}, [], []
        for s in range(STEP):
            roots.append(lax.rsqrt(corner[s][s]))
            scaled = [None if u <= s else corner[s][u] * roots[s] for u in range(STEP)]
            inverse.append(roots[s] * roots[s])
            for t in range(s + 1, STEP):
                ratio[t, s] = scaled[t] * roots[s]
                for u in range(t, STEP):
                    corner[t][u] = corner[t][u] - scaled[t] * scaled[u]
        for s in range(STEP):
            for t in range(s + 1, STEP):
                rows[t] = rows[t] - ratio[t, s] * rows[s]
                sides[t] = sides[t] - ratio[t, s] * sides[s]
        if own + 1 < end:
            solved_rows = [rows[s] * inverse[s] for s in range(STEP)]
            solved_sides = [sides[s] * inverse[s] for s in range(STEP)]
            for i in range(own + 1, end):
                factors = [columns[s][i] for s in range(STEP)]
                for s in range(STEP):
                    for t in range(s + 1, STEP):
                        factors[t] = factors[t] - ratio[t, s] * factors[s]
                left[i] = left[i] - tree([factors[s] * solved_rows[s] for s in range(STEP)])
                right[i] = right[i] - tree([factors[s] * solved_sides[s] for s in range(STEP)])
        for s in range(STEP):
            root = roots[s]
            left[own] = jnp.where(row == s, rows[s] * root, left[own])
            right[own] = jnp.where(row == s, sides[s] * root, right[own])
        if (first + STEP) % PANEL == 0 and first + STEP < BLOCK:
            start = (first + STEP - PANEL) // 8
            upper = jnp.concatenate(left[start:end], axis=0)
            side = jnp.concatenate(right[start:end], axis=0)
            update = dot_exact(upper, jnp.concatenate([upper, side], axis=1))
            for i in range(end, pieces):
                left[i] = left[i] - update[8 * i : 8 * i + 8, :BLOCK]
                right[i] = right[i] - update[8 * i : 8 * i + 8, BLOCK:]
    return right


def eliminate(work, first, last):
    blocks = work.shape[0] // BLOCK
    one = lax.broadcasted_iota(jnp.int32, (BLOCK, BLOCK), 0) == lax.broadcasted_iota(jnp.int32, (BLOCK, BLOCK), 1)

    @pl.loop(first, last)
    def _(j):
        own = pl.ds(pl.multiple_of(j * BLOCK, BLOCK), BLOCK)
        pieces = factor_block(work[own, own])
        work[own, own] = jnp.where(one, 1.0, 0.0).astype(jnp.float32)
        work[own, :] = dot_plain(jnp.concatenate(pieces, axis=0), work[own, :])

        @pl.loop(j + 1, blocks)
        def _(i):
            other = pl.ds(pl.multiple_of(i * BLOCK, BLOCK), BLOCK)
            upper = work[own, other]
            work[other, own] = jnp.zeros((BLOCK, BLOCK), jnp.float32)
            work[other, :] = work[other, :] - dot_rows(upper, work[own, :])


def lower_part(value):
    row = lax.broadcasted_iota(jnp.int32, value.shape, 0)
    return jnp.where(lax.broadcasted_iota(jnp.int32, value.shape, 1) <= row, value, 0.0)


def pairs_of(n):
    return [(0, False)] + [(d, 2 * d == n) for d in range(1, n // 2 + 1)]


def own_pair(r, offset, n):
    if 2 * offset == n:
        low = r % offset
        return low, low + offset
    other = (r + offset) % n
    return jnp.minimum(r, other), jnp.maximum(r, other)


def place_symmetric(matrix, held, n, block):
    for r in range(n):
        row = 0
        for offset, split in pairs_of(n):
            if split:
                i, j = r % offset, r % offset + offset
                height, start = block // 2, r // offset * (block // 2)
            else:
                i, j = min(r, (r + offset) % n), max(r, (r + offset) % n)
                height, start = block, 0
            matrix[i * block + start : i * block + start + height, j * block : (j + 1) * block] = held(
                r, row, height
            )
            row += height
    return row


def first_kernel(n, order, steps, r_ref, *refs):
    held, work, stack = refs[:n], refs[n], refs[n + 1]
    size = work.shape[0]
    r = r_ref[0]
    for value, distance in zip(held, order):
        stack[r ^ distance] = value[...]
    work[...] = jnp.zeros_like(work)
    place_symmetric(work, lambda d, row, height: stack[d, row : row + height, :], n, size // n)
    eliminate(work, 0, steps)


def second_kernel(steps, before_ref, work):
    work[...] = before_ref[...]
    eliminate(work, steps, work.shape[0] // BLOCK)


def last_kernel(n, order, r_ref, *refs):
    held, left_ref = refs[:n], refs[n]
    high_ref, low_ref, scales_ref, stack, whole, cross, work = refs[n + 1 :]
    size = left_ref.shape[0]
    block = size // n
    r = r_ref[0]
    for value, distance in zip(held, order):
        stack[r ^ distance] = value[...]
    corner = place_symmetric(work, lambda d, row, height: stack[d, row : row + height, :], n, block)
    for d in range(n):
        for j in range(n):
            cross[d * block : (d + 1) * block, j * block : (j + 1) * block] = stack[
                d, corner + j * block : corner + (j + 1) * block, :
            ]
    inverse = lower_part(left_ref[...])
    whole[:size, :size] = inverse
    whole[:size, size:] = jnp.zeros((size, size), jnp.float32)
    cross[...] = dot_plain(inverse, cross[...])
    row = lax.broadcasted_iota(jnp.int32, (size, size), 0)
    column = lax.broadcasted_iota(jnp.int32, (size, size), 1)
    upper = jnp.where(row // block <= column // block, work[...], 0.0)
    work[...] = upper - dot_rows(cross[...], cross[...])
    eliminate(work, 0, size // BLOCK)
    inverse = lower_part(work[...])
    whole[size:, size:] = inverse
    whole[size:, :size] = -dot_plain(inverse, dot_rows(cross[...], whole[:size, :size]))
    one = lax.broadcasted_iota(jnp.int32, (BLOCK, BLOCK), 0) == lax.broadcasted_iota(jnp.int32, (BLOCK, BLOCK), 1)
    for first in range(0, 2 * size, BLOCK):
        at = slice(first, first + BLOCK)
        scales_ref[:, at] = 1.0 / jnp.sum(jnp.where(one, whole[at, at], 0.0), axis=0, keepdims=True)
    portion = high_ref.shape[0]
    rows = whole[pl.ds(pl.multiple_of(r * portion, portion), portion), :]
    high = rows.astype(jnp.bfloat16)
    high_ref[...] = high
    low_ref[...] = (rows - high.astype(jnp.float32)).astype(jnp.bfloat16)


VMEM = pl.BlockSpec(memory_space=pltpu.VMEM)
SMEM = pl.BlockSpec(memory_space=pltpu.SMEM)


def kernel_options():
    return {
        "compiler_params": pltpu.CompilerParams(vmem_limit_bytes=40 * 2**20),
        "cost_estimate": pl.CostEstimate(flops=COST, bytes_accessed=0, transcendentals=0),
    }


def begin_factor(index, order, corner, half):
    n = len(order)
    return pl.pallas_call(
        functools.partial(first_kernel, n, order, half // BLOCK // 2),
        out_shape=jax.ShapeDtypeStruct((half, half), jnp.float32),
        in_specs=[SMEM] + [VMEM] * n,
        out_specs=VMEM,
        scratch_shapes=[pltpu.VMEM((n,) + corner[0].shape, jnp.float32)],
        **kernel_options(),
    )(index, *corner)


def go_on_factor(work):
    return pl.pallas_call(
        functools.partial(second_kernel, work.shape[0] // BLOCK // 2),
        out_shape=jax.ShapeDtypeStruct(work.shape, jnp.float32),
        in_specs=[VMEM],
        out_specs=VMEM,
        **kernel_options(),
    )(work)


def end_factor(index, order, rest, work, size):
    n = len(order)
    half = size // 2
    portion = size // n
    return pl.pallas_call(
        functools.partial(last_kernel, n, order),
        out_shape=[
            jax.ShapeDtypeStruct((portion, size), jnp.bfloat16),
            jax.ShapeDtypeStruct((portion, size), jnp.bfloat16),
            jax.ShapeDtypeStruct((1, size), jnp.float32),
        ],
        in_specs=[SMEM] + [VMEM] * (n + 1),
        out_specs=[VMEM] * 3,
        scratch_shapes=[
            pltpu.VMEM((n,) + rest[0].shape, jnp.float32),
            pltpu.VMEM((size, size), jnp.float32),
            pltpu.VMEM((half, half), jnp.float32),
            pltpu.VMEM((half, half), jnp.float32),
        ],
        **kernel_options(),
    )(index, *rest, work)


def multiply_kernel(layout, tile, which_ref, *refs):
    candidates, factor_ref, out_ref = refs[:-6], refs[-6], refs[-5]
    block, weights, block_ready, ready = refs[-4:]
    half = out_ref.shape[2]
    tiles = half // tile
    core = which_ref[0]
    places = []
    for i in range(2 * tiles):
        part = lax.rem(i // tiles + core + 1, 2)
        places.append(pl.ds(pl.multiple_of(part * half + i % tiles * tile, tile), tile))
    first, row = 0, 0
    for piece, count in enumerate(layout):
        height = candidates[first].shape[0]
        for k in range(count):

            @pl.when(which_ref[piece + 1] == k)
            def _(k=k, first=first, row=row, height=height, piece=piece):
                pltpu.make_async_copy(
                    candidates[first + k], block.at[pl.ds(row, height)], block_ready.at[piece]
                ).start()

        first, row = first + count, row + height
    copies = [pltpu.make_async_copy(factor_ref.at[p], weights.at[i], ready.at[i]) for i, p in enumerate(places)]
    for copy in copies:
        copy.start()
    first, row = 0, 0
    for piece, count in enumerate(layout):
        height = candidates[first].shape[0]
        pltpu.make_async_copy(candidates[first], block.at[pl.ds(row, height)], block_ready.at[piece]).wait()
        first, row = first + count, row + height
    for i, copy in enumerate(copies):
        copy.wait()
        out_ref[i // tiles, :, i % tiles * tile : (i % tiles + 1) * tile] = lax.dot_general(
            block[...], weights[i], (((1,), (1,)), ((), ())), preferred_element_type=jnp.float32
        )


def multiply(which, pieces, factor):
    rows, depth = factor.shape
    columns = sum(candidates[0].shape[0] for candidates in pieces)
    half = rows // 2
    tile = next((t for t in (896, 512, 256) if half % t == 0), half)
    tiles = 2 * half // tile
    layout = tuple(len(candidates) for candidates in pieces)
    return pl.pallas_call(
        functools.partial(multiply_kernel, layout, tile),
        in_specs=[pl.BlockSpec(memory_space=pltpu.SMEM)] + [pl.BlockSpec(memory_space=pl.ANY)] * (sum(layout) + 1),
        out_specs=pl.BlockSpec(memory_space=pltpu.VMEM),
        scratch_shapes=[
            pltpu.VMEM((columns, depth), jnp.bfloat16),
            pltpu.VMEM((tiles, tile, depth), jnp.bfloat16),
            pltpu.SemaphoreType.DMA((len(layout),)),
            pltpu.SemaphoreType.DMA((tiles,)),
        ],
        out_shape=jax.ShapeDtypeStruct((2, columns, half), jnp.float32),
        compiler_params=pltpu.CompilerParams(vmem_limit_bytes=40 * 2**20),
        cost_estimate=pl.CostEstimate(flops=COST, bytes_accessed=0, transcendentals=0),
    )(which, *[c for candidates in pieces for c in candidates], factor)


def local(factor, basis_rows):
    rows, depth = factor.shape
    own_basis = basis_rows.shape[0]
    n_row, n_col = lax.axis_size("row"), lax.axis_size("col")
    basis = own_basis * n_col
    half = rows // 2
    index = lax.axis_index("row")
    plane = lax.axis_index("col")
    core = index % 2

    def exchange(value, axis, distance):
        size = lax.axis_size(axis)
        return lax.ppermute(value, axis, [(i, i ^ distance) for i in range(size)])

    rounded = basis_rows.astype(jnp.bfloat16)
    cut = own_basis // 2

    def stream(part):
        below, above = [part], [part]
        for hop in range(1, n_col):
            below.append(lax.ppermute(below[-1], "col", [(i, i + 1) for i in range(hop - 1, n_col - 1)]))
            above.append(lax.ppermute(above[-1], "col", [(i + 1, i) for i in range(0, n_col - hop)]))
        return below, above

    halves = [jnp.zeros((basis, half), jnp.bfloat16)] * 2

    def after(value, *others):
        return lax.optimization_barrier((value, others))[0]

    def begin_unit(pieces, *others):
        which = jnp.stack([core] + [jnp.where(hop <= plane, 0, hop - plane) for hop, _, _ in pieces])
        which = after(which.astype(jnp.int32), *others)
        products = multiply(which, [candidates for _, _, candidates in pieces], factor)
        return products[1] + exchange(products[0], "row", 1)

    def sum_chips(total):
        distance = 2
        while distance < n_row:
            narrow = total.astype(jnp.bfloat16)
            total = narrow.astype(jnp.float32) + exchange(narrow, "row", distance).astype(jnp.float32)
            distance *= 2
        return total.astype(jnp.bfloat16)

    def end_unit(halves, pieces, total):
        other = exchange(total, "row", 1)
        row = 0
        for hop, offset, candidates in pieces:
            height = candidates[0].shape[0]
            start = jnp.where(hop <= plane, plane - hop, hop) * own_basis + offset
            halves = [
                lax.dynamic_update_slice_in_dim(h, v[row : row + height], start, 0)
                for h, v in zip(halves, (total, other))
            ]
            row += height
        return halves

    streams = []
    for offset, part in ((0, rounded[:cut]), (cut, rounded[cut:])):
        below, above = stream(part)
        streams.append([(hop, offset, [below[hop]] + above[1 : hop + 1]) for hop in range(1, n_col)])
    units = [[(0, 0, [rounded])]] + [list(pair) for pair in zip(*streams)]
    units = units[:-1] + [[piece] for piece in units[-1]]
    begun, sums = [], []
    for k, unit in enumerate(units):
        first = [begun[j] for i, j in [(4, 2)] if i == k] + [sums[j] for i, j in [(4, 1)] if i == k]
        begun.append(begin_unit(unit, *first))
        sums.append(sum_chips(begun[-1]))
    for unit, total in zip(units, sums):
        halves = end_unit(halves, unit, total)

    side = basis // 2
    block = side // n_row

    def gram(rows, columns):
        return sum(
            lax.dot_general(
                lax.dynamic_slice_in_dim(h, rows[0], rows[1], 0),
                lax.dynamic_slice_in_dim(h, columns[0], columns[1], 0),
                (((1,), (1,)), ((), ())),
                preferred_element_type=jnp.float32,
            )
            for h in halves
        )

    def share(start):
        found = []
        for offset, split in pairs_of(n_row):
            i, j = own_pair(index, offset, n_row) if offset else (index, index)
            height = block // 2 if split else block
            first = start + i * block + (index // offset * height if split else 0)
            found.append(gram((first, height), (start + j * block, block)))
        return found

    corner = jnp.concatenate(share(0), axis=0)
    cross = gram((index * block, block), (side, side))
    rest = jnp.concatenate(share(side) + [cross[:, j * block : (j + 1) * block] for j in range(n_row)], axis=0)

    def over_planes(value, others):
        if n_col == 4:
            toward = value + lax.ppermute(value, "col", [(0, 1), (3, 2)])
            if others is not None:
                toward = after(toward, others)
            both = toward + lax.ppermute(toward, "col", [(1, 2), (2, 1)])
            outward = lax.ppermute(both, "col", [(1, 0), (2, 3)])
            total = jnp.where((plane == 0) | (plane == 3), outward, both)
            return total, total
        distance = 1
        while distance < n_col:
            value = value + exchange(value, "col", distance)
            distance *= 2
        return value, value

    def over_row(value, *others):
        held = {0: value}
        distances = [1 << k for k in range(1, n_row.bit_length() - 1)] + [1]
        for distance in distances:
            if distance == 1 and others:
                held = {d: after(v, *others) for d, v in held.items()}
            held |= {d ^ distance: exchange(v, "row", distance) for d, v in held.items()}
        return held

    corner, passed = over_planes(corner, None)
    rest, _ = over_planes(rest, passed)
    corner = over_row(corner)
    order = tuple(corner)
    device = index.reshape(1).astype(jnp.int32)
    work = begin_factor(device, order, list(corner.values()), side)
    rest = after(rest, work)
    work = go_on_factor(work)
    rest = over_row(rest, work)
    high, low, scales = end_factor(device, order, list(rest.values()), work, basis)
    first = jnp.where(core == 0, halves[0], halves[1])
    second = jnp.where(core == 0, halves[1], halves[0])
    products = jnp.concatenate([first, second], axis=1)
    new_basis = lax.dot_general(
        products, high, (((0,), (1,)), ((), ())), preferred_element_type=jnp.float32
    ) + lax.dot_general(products, low, (((0,), (1,)), ((), ())), preferred_element_type=jnp.float32)
    return (math.sqrt(ORDER) * new_basis, scales[0])


def solution(mesh):
    return jax.shard_map(
        local,
        mesh=mesh,
        in_specs=(P(("layers", "col"), "row"), P(("layers", "col"), "row")),
        out_specs=(P(("layers", "col"), "row"), P("layers")),
        check_vma=False,
    )
```

```python
import functools
import math

import jax
import jax.numpy as jnp
from jax import lax
from jax.experimental import pallas as pl
from jax.experimental.pallas import tpu as pltpu
from jax.sharding import PartitionSpec as P

ORDER = 14336
BLOCK = 128
STEP = 8
PANEL = 64
EXACT = lax.Precision.HIGHEST
COST = 10**10


def dot_exact(x, y):
    return lax.dot_general(x, y, (((0,), (0,)), ((), ())), precision=EXACT, preferred_element_type=jnp.float32)


def split(x):
    high = x.astype(jnp.bfloat16)
    return high, (x - high.astype(jnp.float32)).astype(jnp.bfloat16)


def dot_split(x, y, dimension):
    (x, x_low), (y, y_low) = split(x), split(y)

    def dot(u, v):
        return lax.dot_general(u, v, (((dimension,), (0,)), ((), ())), preferred_element_type=jnp.float32)

    return dot(x, y) + (dot(x_low, y) + dot(x, y_low))


def dot_rows(x, y):
    return dot_split(x, y, 0)


def dot_plain(x, y):
    return dot_split(x, y, 1)


def tree(terms):
    while len(terms) > 1:
        terms = [a + b for a, b in zip(terms[::2], terms[1::2])]
    return terms[0]


def factor_block(block):
    pieces = BLOCK // 8
    shape = (8, BLOCK)
    row = lax.broadcasted_iota(jnp.int32, shape, 0)
    column = lax.broadcasted_iota(jnp.int32, shape, 1)
    left = [block[8 * i : 8 * i + 8, :] for i in range(pieces)]
    right = [jnp.where(column == row + 8 * i, 1.0, 0.0).astype(jnp.float32) for i in range(pieces)]

    def spread(value):
        return jnp.broadcast_to(value, shape)

    for first in range(0, BLOCK, STEP):
        own = first // 8
        end = (first // PANEL + 1) * PANEL // 8
        lanes = [spread(left[own][:, first + s : first + s + 1]) for s in range(STEP)]
        corner = [[spread(lanes[t][s : s + 1, :]) if t >= s else None for t in range(STEP)] for s in range(STEP)]
        rows = [spread(left[own][s : s + 1, :]) for s in range(STEP)]
        sides = [spread(right[own][s : s + 1, :]) for s in range(STEP)]
        columns = [
            {i: spread(left[i][:, first + s : first + s + 1]) for i in range(own + 1, end)} for s in range(STEP)
        ]
        ratio, inverse, roots = {}, [], []
        for s in range(STEP):
            roots.append(lax.rsqrt(corner[s][s]))
            scaled = [None if u <= s else corner[s][u] * roots[s] for u in range(STEP)]
            inverse.append(roots[s] * roots[s])
            for t in range(s + 1, STEP):
                ratio[t, s] = scaled[t] * roots[s]
                for u in range(t, STEP):
                    corner[t][u] = corner[t][u] - scaled[t] * scaled[u]
        for s in range(STEP):
            for t in range(s + 1, STEP):
                rows[t] = rows[t] - ratio[t, s] * rows[s]
                sides[t] = sides[t] - ratio[t, s] * sides[s]
        if own + 1 < end:
            solved_rows = [rows[s] * inverse[s] for s in range(STEP)]
            solved_sides = [sides[s] * inverse[s] for s in range(STEP)]
            for i in range(own + 1, end):
                factors = [columns[s][i] for s in range(STEP)]
                for s in range(STEP):
                    for t in range(s + 1, STEP):
                        factors[t] = factors[t] - ratio[t, s] * factors[s]
                left[i] = left[i] - tree([factors[s] * solved_rows[s] for s in range(STEP)])
                right[i] = right[i] - tree([factors[s] * solved_sides[s] for s in range(STEP)])
        for s in range(STEP):
            root = roots[s]
            left[own] = jnp.where(row == s, rows[s] * root, left[own])
            right[own] = jnp.where(row == s, sides[s] * root, right[own])
        if (first + STEP) % PANEL == 0 and first + STEP < BLOCK:
            start = (first + STEP - PANEL) // 8
            upper = jnp.concatenate(left[start:end], axis=0)
            side = jnp.concatenate(right[start:end], axis=0)
            update = dot_exact(upper, jnp.concatenate([upper, side], axis=1))
            for i in range(end, pieces):
                left[i] = left[i] - update[8 * i : 8 * i + 8, :BLOCK]
                right[i] = right[i] - update[8 * i : 8 * i + 8, BLOCK:]
    return right


def eliminate(work, first, last):
    blocks = work.shape[0] // BLOCK
    one = lax.broadcasted_iota(jnp.int32, (BLOCK, BLOCK), 0) == lax.broadcasted_iota(jnp.int32, (BLOCK, BLOCK), 1)

    @pl.loop(first, last)
    def _(j):
        own = pl.ds(pl.multiple_of(j * BLOCK, BLOCK), BLOCK)
        pieces = factor_block(work[own, own])
        work[own, own] = jnp.where(one, 1.0, 0.0).astype(jnp.float32)
        work[own, :] = dot_plain(jnp.concatenate(pieces, axis=0), work[own, :])

        @pl.loop(j + 1, blocks)
        def _(i):
            other = pl.ds(pl.multiple_of(i * BLOCK, BLOCK), BLOCK)
            upper = work[own, other]
            work[other, own] = jnp.zeros((BLOCK, BLOCK), jnp.float32)
            work[other, :] = work[other, :] - dot_rows(upper, work[own, :])


def lower_part(value):
    row = lax.broadcasted_iota(jnp.int32, value.shape, 0)
    return jnp.where(lax.broadcasted_iota(jnp.int32, value.shape, 1) <= row, value, 0.0)


def pairs_of(n):
    return [(0, False)] + [(d, 2 * d == n) for d in range(1, n // 2 + 1)]


def own_pair(r, offset, n):
    if 2 * offset == n:
        low = r % offset
        return low, low + offset
    other = (r + offset) % n
    return jnp.minimum(r, other), jnp.maximum(r, other)


def place_symmetric(matrix, held, n, block):
    for r in range(n):
        row = 0
        for offset, split in pairs_of(n):
            if split:
                i, j = r % offset, r % offset + offset
                height, start = block // 2, r // offset * (block // 2)
            else:
                i, j = min(r, (r + offset) % n), max(r, (r + offset) % n)
                height, start = block, 0
            matrix[i * block + start : i * block + start + height, j * block : (j + 1) * block] = held(
                r, row, height
            )
            row += height
    return row


def first_kernel(n, order, steps, r_ref, *refs):
    held, work, stack = refs[:n], refs[n], refs[n + 1]
    size = work.shape[0]
    r = r_ref[0]
    for value, distance in zip(held, order):
        stack[r ^ distance] = value[...]
    work[...] = jnp.zeros_like(work)
    place_symmetric(work, lambda d, row, height: stack[d, row : row + height, :], n, size // n)
    eliminate(work, 0, steps)


def second_kernel(steps, before_ref, work):
    work[...] = before_ref[...]
    eliminate(work, steps, work.shape[0] // BLOCK)


def last_kernel(n, order, r_ref, *refs):
    held, left_ref = refs[:n], refs[n]
    high_ref, low_ref, scales_ref, stack, whole, cross, work = refs[n + 1 :]
    size = left_ref.shape[0]
    block = size // n
    r = r_ref[0]
    for value, distance in zip(held, order):
        stack[r ^ distance] = value[...]
    corner = place_symmetric(work, lambda d, row, height: stack[d, row : row + height, :], n, block)
    for d in range(n):
        for j in range(n):
            cross[d * block : (d + 1) * block, j * block : (j + 1) * block] = stack[
                d, corner + j * block : corner + (j + 1) * block, :
            ]
    inverse = lower_part(left_ref[...])
    whole[:size, :size] = inverse
    whole[:size, size:] = jnp.zeros((size, size), jnp.float32)
    cross[...] = dot_plain(inverse, cross[...])
    row = lax.broadcasted_iota(jnp.int32, (size, size), 0)
    column = lax.broadcasted_iota(jnp.int32, (size, size), 1)
    upper = jnp.where(row // block <= column // block, work[...], 0.0)
    work[...] = upper - dot_rows(cross[...], cross[...])
    eliminate(work, 0, size // BLOCK)
    inverse = lower_part(work[...])
    whole[size:, size:] = inverse
    whole[size:, :size] = -dot_plain(inverse, dot_rows(cross[...], whole[:size, :size]))
    one = lax.broadcasted_iota(jnp.int32, (BLOCK, BLOCK), 0) == lax.broadcasted_iota(jnp.int32, (BLOCK, BLOCK), 1)
    for first in range(0, 2 * size, BLOCK):
        at = slice(first, first + BLOCK)
        scales_ref[:, at] = 1.0 / jnp.sum(jnp.where(one, whole[at, at], 0.0), axis=0, keepdims=True)
    portion = high_ref.shape[0]
    rows = whole[pl.ds(pl.multiple_of(r * portion, portion), portion), :]
    high = rows.astype(jnp.bfloat16)
    high_ref[...] = high
    low_ref[...] = (rows - high.astype(jnp.float32)).astype(jnp.bfloat16)


VMEM = pl.BlockSpec(memory_space=pltpu.VMEM)
SMEM = pl.BlockSpec(memory_space=pltpu.SMEM)


def kernel_options():
    return {
        "compiler_params": pltpu.CompilerParams(vmem_limit_bytes=40 * 2**20),
        "cost_estimate": pl.CostEstimate(flops=COST, bytes_accessed=0, transcendentals=0),
    }


def begin_factor(index, order, corner, half):
    n = len(order)
    return pl.pallas_call(
        functools.partial(first_kernel, n, order, half // BLOCK // 2),
        out_shape=jax.ShapeDtypeStruct((half, half), jnp.float32),
        in_specs=[SMEM] + [VMEM] * n,
        out_specs=VMEM,
        scratch_shapes=[pltpu.VMEM((n,) + corner[0].shape, jnp.float32)],
        **kernel_options(),
    )(index, *corner)


def go_on_factor(work):
    return pl.pallas_call(
        functools.partial(second_kernel, work.shape[0] // BLOCK // 2),
        out_shape=jax.ShapeDtypeStruct(work.shape, jnp.float32),
        in_specs=[VMEM],
        out_specs=VMEM,
        **kernel_options(),
    )(work)


def end_factor(index, order, rest, work, size):
    n = len(order)
    half = size // 2
    portion = size // n
    return pl.pallas_call(
        functools.partial(last_kernel, n, order),
        out_shape=[
            jax.ShapeDtypeStruct((portion, size), jnp.bfloat16),
            jax.ShapeDtypeStruct((portion, size), jnp.bfloat16),
            jax.ShapeDtypeStruct((1, size), jnp.float32),
        ],
        in_specs=[SMEM] + [VMEM] * (n + 1),
        out_specs=[VMEM] * 3,
        scratch_shapes=[
            pltpu.VMEM((n,) + rest[0].shape, jnp.float32),
            pltpu.VMEM((size, size), jnp.float32),
            pltpu.VMEM((half, half), jnp.float32),
            pltpu.VMEM((half, half), jnp.float32),
        ],
        **kernel_options(),
    )(index, *rest, work)


def multiply_kernel(layout, tile, which_ref, *refs):
    candidates, factor_ref, out_ref = refs[:-6], refs[-6], refs[-5]
    block, weights, block_ready, ready = refs[-4:]
    half = out_ref.shape[2]
    tiles = half // tile
    core = which_ref[0]
    places = []
    for i in range(2 * tiles):
        part = lax.rem(i // tiles + core + 1, 2)
        places.append(pl.ds(pl.multiple_of(part * half + i % tiles * tile, tile), tile))
    first, row = 0, 0
    for piece, count in enumerate(layout):
        height = candidates[first].shape[0]
        for k in range(count):

            @pl.when(which_ref[piece + 1] == k)
            def _(k=k, first=first, row=row, height=height, piece=piece):
                pltpu.make_async_copy(
                    candidates[first + k], block.at[pl.ds(row, height)], block_ready.at[piece]
                ).start()

        first, row = first + count, row + height
    copies = [pltpu.make_async_copy(factor_ref.at[p], weights.at[i], ready.at[i]) for i, p in enumerate(places)]
    for copy in copies:
        copy.start()
    first, row = 0, 0
    for piece, count in enumerate(layout):
        height = candidates[first].shape[0]
        pltpu.make_async_copy(candidates[first], block.at[pl.ds(row, height)], block_ready.at[piece]).wait()
        first, row = first + count, row + height
    for i, copy in enumerate(copies):
        copy.wait()
        out_ref[i // tiles, :, i % tiles * tile : (i % tiles + 1) * tile] = lax.dot_general(
            block[...], weights[i], (((1,), (1,)), ((), ())), preferred_element_type=jnp.float32
        )


def multiply(which, pieces, factor):
    rows, depth = factor.shape
    columns = sum(candidates[0].shape[0] for candidates in pieces)
    half = rows // 2
    tile = next((t for t in (896, 512, 256) if half % t == 0), half)
    tiles = 2 * half // tile
    layout = tuple(len(candidates) for candidates in pieces)
    return pl.pallas_call(
        functools.partial(multiply_kernel, layout, tile),
        in_specs=[pl.BlockSpec(memory_space=pltpu.SMEM)] + [pl.BlockSpec(memory_space=pl.ANY)] * (sum(layout) + 1),
        out_specs=pl.BlockSpec(memory_space=pltpu.VMEM),
        scratch_shapes=[
            pltpu.VMEM((columns, depth), jnp.bfloat16),
            pltpu.VMEM((tiles, tile, depth), jnp.bfloat16),
            pltpu.SemaphoreType.DMA((len(layout),)),
            pltpu.SemaphoreType.DMA((tiles,)),
        ],
        out_shape=jax.ShapeDtypeStruct((2, columns, half), jnp.float32),
        compiler_params=pltpu.CompilerParams(vmem_limit_bytes=40 * 2**20),
        cost_estimate=pl.CostEstimate(flops=COST, bytes_accessed=0, transcendentals=0),
    )(which, *[c for candidates in pieces for c in candidates], factor)


def local(factor, basis_rows):
    rows, depth = factor.shape
    own_basis = basis_rows.shape[0]
    n_row, n_col = lax.axis_size("row"), lax.axis_size("col")
    basis = own_basis * n_col
    half = rows // 2
    index = lax.axis_index("row")
    plane = lax.axis_index("col")
    core = index % 2

    def exchange(value, axis, distance):
        size = lax.axis_size(axis)
        return lax.ppermute(value, axis, [(i, i ^ distance) for i in range(size)])

    rounded = basis_rows.astype(jnp.bfloat16)
    cut = own_basis // 2

    def stream(part):
        below, above = [part], [part]
        for hop in range(1, n_col):
            below.append(lax.ppermute(below[-1], "col", [(i, i + 1) for i in range(hop - 1, n_col - 1)]))
            above.append(lax.ppermute(above[-1], "col", [(i + 1, i) for i in range(0, n_col - hop)]))
        return below, above

    halves = [jnp.zeros((basis, half), jnp.bfloat16)] * 2

    def after(value, *others):
        return lax.optimization_barrier((value, others))[0]

    def begin_unit(pieces, *others):
        which = jnp.stack([core] + [jnp.where(hop <= plane, 0, hop - plane) for hop, _, _ in pieces])
        which = after(which.astype(jnp.int32), *others)
        products = multiply(which, [candidates for _, _, candidates in pieces], factor)
        return products[1] + exchange(products[0], "row", 1)

    def sum_chips(total):
        distance = 2
        while distance < n_row:
            narrow = total.astype(jnp.bfloat16)
            total = narrow.astype(jnp.float32) + exchange(narrow, "row", distance).astype(jnp.float32)
            distance *= 2
        return total.astype(jnp.bfloat16)

    def end_unit(halves, pieces, total):
        other = exchange(total, "row", 1)
        row = 0
        for hop, offset, candidates in pieces:
            height = candidates[0].shape[0]
            start = jnp.where(hop <= plane, plane - hop, hop) * own_basis + offset
            halves = [
                lax.dynamic_update_slice_in_dim(h, v[row : row + height], start, 0)
                for h, v in zip(halves, (total, other))
            ]
            row += height
        return halves

    streams = []
    for offset, part in ((0, rounded[:cut]), (cut, rounded[cut:])):
        below, above = stream(part)
        streams.append([(hop, offset, [below[hop]] + above[1 : hop + 1]) for hop in range(1, n_col)])
    units = [[(0, 0, [rounded])]] + [list(pair) for pair in zip(*streams)]
    units = units[:-1] + [[piece] for piece in units[-1]]
    begun, sums = [], []
    for k, unit in enumerate(units):
        first = [begun[k - 2]] if k == len(units) - 1 else []
        begun.append(begin_unit(unit, *first))
        sums.append(sum_chips(begun[-1]))
    for unit, total in zip(units, sums):
        halves = end_unit(halves, unit, total)

    side = basis // 2
    block = side // n_row

    def gram(rows, columns):
        return sum(
            lax.dot_general(
                lax.dynamic_slice_in_dim(h, rows[0], rows[1], 0),
                lax.dynamic_slice_in_dim(h, columns[0], columns[1], 0),
                (((1,), (1,)), ((), ())),
                preferred_element_type=jnp.float32,
            )
            for h in halves
        )

    def share(start):
        found = []
        for offset, split in pairs_of(n_row):
            i, j = own_pair(index, offset, n_row) if offset else (index, index)
            height = block // 2 if split else block
            first = start + i * block + (index // offset * height if split else 0)
            found.append(gram((first, height), (start + j * block, block)))
        return found

    corner = jnp.concatenate(share(0), axis=0)
    cross = gram((index * block, block), (side, side))
    rest = jnp.concatenate(share(side) + [cross[:, j * block : (j + 1) * block] for j in range(n_row)], axis=0)

    def over_planes(value, others):
        if n_col == 4:
            toward = value + lax.ppermute(value, "col", [(0, 1), (3, 2)])
            if others is not None:
                toward = after(toward, others)
            both = toward + lax.ppermute(toward, "col", [(1, 2), (2, 1)])
            outward = lax.ppermute(both, "col", [(1, 0), (2, 3)])
            total = jnp.where((plane == 0) | (plane == 3), outward, both)
            return total, total
        distance = 1
        while distance < n_col:
            value = value + exchange(value, "col", distance)
            distance *= 2
        return value, value

    def over_row(value, *others):
        held = {0: value}
        distances = [1 << k for k in range(1, n_row.bit_length() - 1)] + [1]
        for distance in distances:
            if distance == 1 and others:
                held = {d: after(v, *others) for d, v in held.items()}
            held |= {d ^ distance: exchange(v, "row", distance) for d, v in held.items()}
        return held

    corner, passed = over_planes(corner, None)
    rest, _ = over_planes(rest, passed)
    corner = over_row(corner)
    order = tuple(corner)
    device = index.reshape(1).astype(jnp.int32)
    work = begin_factor(device, order, list(corner.values()), side)
    rest = after(rest, work)
    work = go_on_factor(work)
    rest = over_row(rest, work)
    high, low, scales = end_factor(device, order, list(rest.values()), work, basis)
    first = jnp.where(core == 0, halves[0], halves[1])
    second = jnp.where(core == 0, halves[1], halves[0])
    products = jnp.concatenate([first, second], axis=1)
    new_basis = lax.dot_general(
        products, high, (((0,), (1,)), ((), ())), preferred_element_type=jnp.float32
    ) + lax.dot_general(products, low, (((0,), (1,)), ((), ())), preferred_element_type=jnp.float32)
    return (math.sqrt(ORDER) * new_basis, scales[0])


def solution(mesh):
    return jax.shard_map(
        local,
        mesh=mesh,
        in_specs=(P(("layers", "col"), "row"), P(("layers", "col"), "row")),
        out_specs=(P(("layers", "col"), "row"), P("layers")),
        check_vma=False,
    )
```

```python
import functools
import math

import jax
import jax.numpy as jnp
from jax import lax
from jax.experimental import pallas as pl
from jax.experimental.pallas import tpu as pltpu
from jax.sharding import PartitionSpec as P

ORDER = 14336
BLOCK = 128
STEP = 8
PANEL = 64
EXACT = lax.Precision.HIGHEST
COST = 10**10


def dot_exact(x, y):
    return lax.dot_general(x, y, (((0,), (0,)), ((), ())), precision=EXACT, preferred_element_type=jnp.float32)


def split(x):
    high = x.astype(jnp.bfloat16)
    return high, (x - high.astype(jnp.float32)).astype(jnp.bfloat16)


def dot_split(x, y, dimension):
    (x, x_low), (y, y_low) = split(x), split(y)

    def dot(u, v):
        return lax.dot_general(u, v, (((dimension,), (0,)), ((), ())), preferred_element_type=jnp.float32)

    return dot(x, y) + (dot(x_low, y) + dot(x, y_low))


def dot_rows(x, y):
    return dot_split(x, y, 0)


def dot_plain(x, y):
    return dot_split(x, y, 1)


def tree(terms):
    while len(terms) > 1:
        terms = [a + b for a, b in zip(terms[::2], terms[1::2])]
    return terms[0]


def factor_block(block):
    pieces = BLOCK // 8
    shape = (8, BLOCK)
    row = lax.broadcasted_iota(jnp.int32, shape, 0)
    column = lax.broadcasted_iota(jnp.int32, shape, 1)
    left = [block[8 * i : 8 * i + 8, :] for i in range(pieces)]
    right = [jnp.where(column == row + 8 * i, 1.0, 0.0).astype(jnp.float32) for i in range(pieces)]

    def spread(value):
        return jnp.broadcast_to(value, shape)

    for first in range(0, BLOCK, STEP):
        own = first // 8
        end = (first // PANEL + 1) * PANEL // 8
        lanes = [spread(left[own][:, first + s : first + s + 1]) for s in range(STEP)]
        corner = [[spread(lanes[t][s : s + 1, :]) if t >= s else None for t in range(STEP)] for s in range(STEP)]
        rows = [spread(left[own][s : s + 1, :]) for s in range(STEP)]
        sides = [spread(right[own][s : s + 1, :]) for s in range(STEP)]
        columns = [
            {i: spread(left[i][:, first + s : first + s + 1]) for i in range(own + 1, end)} for s in range(STEP)
        ]
        ratio, inverse, roots = {}, [], []
        for s in range(STEP):
            roots.append(lax.rsqrt(corner[s][s]))
            scaled = [None if u <= s else corner[s][u] * roots[s] for u in range(STEP)]
            inverse.append(roots[s] * roots[s])
            for t in range(s + 1, STEP):
                ratio[t, s] = scaled[t] * roots[s]
                for u in range(t, STEP):
                    corner[t][u] = corner[t][u] - scaled[t] * scaled[u]
        for s in range(STEP):
            for t in range(s + 1, STEP):
                rows[t] = rows[t] - ratio[t, s] * rows[s]
                sides[t] = sides[t] - ratio[t, s] * sides[s]
        if own + 1 < end:
            solved_rows = [rows[s] * inverse[s] for s in range(STEP)]
            solved_sides = [sides[s] * inverse[s] for s in range(STEP)]
            for i in range(own + 1, end):
                factors = [columns[s][i] for s in range(STEP)]
                for s in range(STEP):
                    for t in range(s + 1, STEP):
                        factors[t] = factors[t] - ratio[t, s] * factors[s]
                left[i] = left[i] - tree([factors[s] * solved_rows[s] for s in range(STEP)])
                right[i] = right[i] - tree([factors[s] * solved_sides[s] for s in range(STEP)])
        for s in range(STEP):
            root = roots[s]
            left[own] = jnp.where(row == s, rows[s] * root, left[own])
            right[own] = jnp.where(row == s, sides[s] * root, right[own])
        if (first + STEP) % PANEL == 0 and first + STEP < BLOCK:
            start = (first + STEP - PANEL) // 8
            upper = jnp.concatenate(left[start:end], axis=0)
            side = jnp.concatenate(right[start:end], axis=0)
            update = dot_exact(upper, jnp.concatenate([upper, side], axis=1))
            for i in range(end, pieces):
                left[i] = left[i] - update[8 * i : 8 * i + 8, :BLOCK]
                right[i] = right[i] - update[8 * i : 8 * i + 8, BLOCK:]
    return right


def eliminate(work, first, last):
    blocks = work.shape[0] // BLOCK
    one = lax.broadcasted_iota(jnp.int32, (BLOCK, BLOCK), 0) == lax.broadcasted_iota(jnp.int32, (BLOCK, BLOCK), 1)

    @pl.loop(first, last)
    def _(j):
        own = pl.ds(pl.multiple_of(j * BLOCK, BLOCK), BLOCK)
        pieces = factor_block(work[own, own])
        work[own, own] = jnp.where(one, 1.0, 0.0).astype(jnp.float32)
        work[own, :] = dot_plain(jnp.concatenate(pieces, axis=0), work[own, :])

        @pl.loop(j + 1, blocks)
        def _(i):
            other = pl.ds(pl.multiple_of(i * BLOCK, BLOCK), BLOCK)
            upper = work[own, other]
            work[other, own] = jnp.zeros((BLOCK, BLOCK), jnp.float32)
            work[other, :] = work[other, :] - dot_rows(upper, work[own, :])


def lower_part(value):
    row = lax.broadcasted_iota(jnp.int32, value.shape, 0)
    return jnp.where(lax.broadcasted_iota(jnp.int32, value.shape, 1) <= row, value, 0.0)


def pairs_of(n):
    return [(0, False)] + [(d, 2 * d == n) for d in range(1, n // 2 + 1)]


def own_pair(r, offset, n):
    if 2 * offset == n:
        low = r % offset
        return low, low + offset
    other = (r + offset) % n
    return jnp.minimum(r, other), jnp.maximum(r, other)


def place_symmetric(matrix, held, n, block):
    for r in range(n):
        row = 0
        for offset, split in pairs_of(n):
            if split:
                i, j = r % offset, r % offset + offset
                height, start = block // 2, r // offset * (block // 2)
            else:
                i, j = min(r, (r + offset) % n), max(r, (r + offset) % n)
                height, start = block, 0
            matrix[i * block + start : i * block + start + height, j * block : (j + 1) * block] = held(
                r, row, height
            )
            row += height
    return row


def first_kernel(n, order, steps, r_ref, *refs):
    held, work, stack = refs[:n], refs[n], refs[n + 1]
    size = work.shape[0]
    r = r_ref[0]
    for value, distance in zip(held, order):
        stack[r ^ distance] = value[...]
    work[...] = jnp.zeros_like(work)
    place_symmetric(work, lambda d, row, height: stack[d, row : row + height, :], n, size // n)
    eliminate(work, 0, steps)


def second_kernel(steps, before_ref, work):
    work[...] = before_ref[...]
    eliminate(work, steps, work.shape[0] // BLOCK)


def last_kernel(n, order, r_ref, *refs):
    held, left_ref = refs[:n], refs[n]
    high_ref, low_ref, scales_ref, stack, whole, cross, work = refs[n + 1 :]
    size = left_ref.shape[0]
    block = size // n
    r = r_ref[0]
    for value, distance in zip(held, order):
        stack[r ^ distance] = value[...]
    corner = place_symmetric(work, lambda d, row, height: stack[d, row : row + height, :], n, block)
    for d in range(n):
        for j in range(n):
            cross[d * block : (d + 1) * block, j * block : (j + 1) * block] = stack[
                d, corner + j * block : corner + (j + 1) * block, :
            ]
    inverse = lower_part(left_ref[...])
    whole[:size, :size] = inverse
    whole[:size, size:] = jnp.zeros((size, size), jnp.float32)
    cross[...] = dot_plain(inverse, cross[...])
    row = lax.broadcasted_iota(jnp.int32, (size, size), 0)
    column = lax.broadcasted_iota(jnp.int32, (size, size), 1)
    upper = jnp.where(row // block <= column // block, work[...], 0.0)
    work[...] = upper - dot_rows(cross[...], cross[...])
    eliminate(work, 0, size // BLOCK)
    inverse = lower_part(work[...])
    whole[size:, size:] = inverse
    portion = high_ref.shape[0]
    start = size + lax.rem(r, n // 2) * portion
    mine = pl.ds(pl.multiple_of(start, portion), portion)
    share = dot_split(whole[mine, size:], cross[...].T, 1)
    whole[mine, :size] = -dot_plain(share, whole[:size, :size])
    one = lax.broadcasted_iota(jnp.int32, (BLOCK, BLOCK), 0) == lax.broadcasted_iota(jnp.int32, (BLOCK, BLOCK), 1)
    for first in range(0, 2 * size, BLOCK):
        at = slice(first, first + BLOCK)
        scales_ref[:, at] = 1.0 / jnp.sum(jnp.where(one, whole[at, at], 0.0), axis=0, keepdims=True)
    rows = whole[pl.ds(pl.multiple_of(r * portion, portion), portion), :]
    high = rows.astype(jnp.bfloat16)
    high_ref[...] = high
    low_ref[...] = (rows - high.astype(jnp.float32)).astype(jnp.bfloat16)


VMEM = pl.BlockSpec(memory_space=pltpu.VMEM)
SMEM = pl.BlockSpec(memory_space=pltpu.SMEM)


def kernel_options():
    return {
        "compiler_params": pltpu.CompilerParams(vmem_limit_bytes=40 * 2**20),
        "cost_estimate": pl.CostEstimate(flops=COST, bytes_accessed=0, transcendentals=0),
    }


def begin_factor(index, order, corner, half):
    n = len(order)
    return pl.pallas_call(
        functools.partial(first_kernel, n, order, half // BLOCK // 2),
        out_shape=jax.ShapeDtypeStruct((half, half), jnp.float32),
        in_specs=[SMEM] + [VMEM] * n,
        out_specs=VMEM,
        scratch_shapes=[pltpu.VMEM((n,) + corner[0].shape, jnp.float32)],
        **kernel_options(),
    )(index, *corner)


def go_on_factor(work):
    return pl.pallas_call(
        functools.partial(second_kernel, work.shape[0] // BLOCK // 2),
        out_shape=jax.ShapeDtypeStruct(work.shape, jnp.float32),
        in_specs=[VMEM],
        out_specs=VMEM,
        **kernel_options(),
    )(work)


def end_factor(index, order, rest, work, size):
    n = len(order)
    half = size // 2
    portion = size // n
    return pl.pallas_call(
        functools.partial(last_kernel, n, order),
        out_shape=[
            jax.ShapeDtypeStruct((portion, size), jnp.bfloat16),
            jax.ShapeDtypeStruct((portion, size), jnp.bfloat16),
            jax.ShapeDtypeStruct((1, size), jnp.float32),
        ],
        in_specs=[SMEM] + [VMEM] * (n + 1),
        out_specs=[VMEM] * 3,
        scratch_shapes=[
            pltpu.VMEM((n,) + rest[0].shape, jnp.float32),
            pltpu.VMEM((size, size), jnp.float32),
            pltpu.VMEM((half, half), jnp.float32),
            pltpu.VMEM((half, half), jnp.float32),
        ],
        **kernel_options(),
    )(index, *rest, work)


def multiply_kernel(layout, tile, which_ref, *refs):
    candidates, factor_ref, out_ref = refs[:-6], refs[-6], refs[-5]
    block, weights, block_ready, ready = refs[-4:]
    half = out_ref.shape[2]
    tiles = half // tile
    core = which_ref[0]
    places = []
    for i in range(2 * tiles):
        part = lax.rem(i // tiles + core + 1, 2)
        places.append(pl.ds(pl.multiple_of(part * half + i % tiles * tile, tile), tile))
    first, row = 0, 0
    for piece, count in enumerate(layout):
        height = candidates[first].shape[0]
        for k in range(count):

            @pl.when(which_ref[piece + 1] == k)
            def _(k=k, first=first, row=row, height=height, piece=piece):
                pltpu.make_async_copy(
                    candidates[first + k], block.at[pl.ds(row, height)], block_ready.at[piece]
                ).start()

        first, row = first + count, row + height
    copies = [pltpu.make_async_copy(factor_ref.at[p], weights.at[i], ready.at[i]) for i, p in enumerate(places)]
    for copy in copies:
        copy.start()
    first, row = 0, 0
    for piece, count in enumerate(layout):
        height = candidates[first].shape[0]
        pltpu.make_async_copy(candidates[first], block.at[pl.ds(row, height)], block_ready.at[piece]).wait()
        first, row = first + count, row + height
    for i, copy in enumerate(copies):
        copy.wait()
        out_ref[i // tiles, :, i % tiles * tile : (i % tiles + 1) * tile] = lax.dot_general(
            block[...], weights[i], (((1,), (1,)), ((), ())), preferred_element_type=jnp.float32
        )


def multiply(which, pieces, factor):
    rows, depth = factor.shape
    columns = sum(candidates[0].shape[0] for candidates in pieces)
    half = rows // 2
    tile = next((t for t in (896, 512, 256) if half % t == 0), half)
    tiles = 2 * half // tile
    layout = tuple(len(candidates) for candidates in pieces)
    return pl.pallas_call(
        functools.partial(multiply_kernel, layout, tile),
        in_specs=[pl.BlockSpec(memory_space=pltpu.SMEM)] + [pl.BlockSpec(memory_space=pl.ANY)] * (sum(layout) + 1),
        out_specs=pl.BlockSpec(memory_space=pltpu.VMEM),
        scratch_shapes=[
            pltpu.VMEM((columns, depth), jnp.bfloat16),
            pltpu.VMEM((tiles, tile, depth), jnp.bfloat16),
            pltpu.SemaphoreType.DMA((len(layout),)),
            pltpu.SemaphoreType.DMA((tiles,)),
        ],
        out_shape=jax.ShapeDtypeStruct((2, columns, half), jnp.float32),
        compiler_params=pltpu.CompilerParams(vmem_limit_bytes=40 * 2**20),
        cost_estimate=pl.CostEstimate(flops=COST, bytes_accessed=0, transcendentals=0),
    )(which, *[c for candidates in pieces for c in candidates], factor)


def local(factor, basis_rows):
    rows, depth = factor.shape
    own_basis = basis_rows.shape[0]
    n_row, n_col = lax.axis_size("row"), lax.axis_size("col")
    basis = own_basis * n_col
    half = rows // 2
    index = lax.axis_index("row")
    plane = lax.axis_index("col")
    core = index % 2

    def exchange(value, axis, distance):
        size = lax.axis_size(axis)
        return lax.ppermute(value, axis, [(i, i ^ distance) for i in range(size)])

    rounded = basis_rows.astype(jnp.bfloat16)
    cut = own_basis // 2

    def stream(part):
        below, above = [part], [part]
        for hop in range(1, n_col):
            below.append(lax.ppermute(below[-1], "col", [(i, i + 1) for i in range(hop - 1, n_col - 1)]))
            above.append(lax.ppermute(above[-1], "col", [(i + 1, i) for i in range(0, n_col - hop)]))
        return below, above

    halves = [jnp.zeros((basis, half), jnp.bfloat16)] * 2

    def after(value, *others):
        return lax.optimization_barrier((value, others))[0]

    def begin_unit(pieces, *others):
        which = jnp.stack([core] + [jnp.where(hop <= plane, 0, hop - plane) for hop, _, _ in pieces])
        which = after(which.astype(jnp.int32), *others)
        products = multiply(which, [candidates for _, _, candidates in pieces], factor)
        return products[1] + exchange(products[0], "row", 1)

    def sum_chips(total):
        distance = 2
        while distance < n_row:
            narrow = total.astype(jnp.bfloat16)
            total = narrow.astype(jnp.float32) + exchange(narrow, "row", distance).astype(jnp.float32)
            distance *= 2
        return total.astype(jnp.bfloat16)

    def end_unit(halves, pieces, total):
        other = exchange(total, "row", 1)
        row = 0
        for hop, offset, candidates in pieces:
            height = candidates[0].shape[0]
            start = jnp.where(hop <= plane, plane - hop, hop) * own_basis + offset
            halves = [
                lax.dynamic_update_slice_in_dim(h, v[row : row + height], start, 0)
                for h, v in zip(halves, (total, other))
            ]
            row += height
        return halves

    streams = []
    for offset, part in ((0, rounded[:cut]), (cut, rounded[cut:])):
        below, above = stream(part)
        streams.append([(hop, offset, [below[hop]] + above[1 : hop + 1]) for hop in range(1, n_col)])
    units = [[(0, 0, [rounded])]] + [list(pair) for pair in zip(*streams)]
    units = units[:-1] + [[piece] for piece in units[-1]]
    begun, sums = [], []
    for k, unit in enumerate(units):
        first = [begun[k - 2]] if k == len(units) - 1 else []
        begun.append(begin_unit(unit, *first))
        sums.append(sum_chips(begun[-1]))
    for unit, total in zip(units, sums):
        halves = end_unit(halves, unit, total)

    side = basis // 2
    block = side // n_row

    def gram(rows, columns):
        return sum(
            lax.dot_general(
                lax.dynamic_slice_in_dim(h, rows[0], rows[1], 0),
                lax.dynamic_slice_in_dim(h, columns[0], columns[1], 0),
                (((1,), (1,)), ((), ())),
                preferred_element_type=jnp.float32,
            )
            for h in halves
        )

    def share(start):
        found = []
        for offset, split in pairs_of(n_row):
            i, j = own_pair(index, offset, n_row) if offset else (index, index)
            height = block // 2 if split else block
            first = start + i * block + (index // offset * height if split else 0)
            found.append(gram((first, height), (start + j * block, block)))
        return found

    corner = jnp.concatenate(share(0), axis=0)
    cross = gram((index * block, block), (side, side))
    rest = jnp.concatenate(share(side) + [cross[:, j * block : (j + 1) * block] for j in range(n_row)], axis=0)

    def over_planes(value, others):
        if n_col == 4:
            toward = value + lax.ppermute(value, "col", [(0, 1), (3, 2)])
            if others is not None:
                toward = after(toward, others)
            both = toward + lax.ppermute(toward, "col", [(1, 2), (2, 1)])
            outward = lax.ppermute(both, "col", [(1, 0), (2, 3)])
            total = jnp.where((plane == 0) | (plane == 3), outward, both)
            return total, total
        distance = 1
        while distance < n_col:
            value = value + exchange(value, "col", distance)
            distance *= 2
        return value, value

    def over_row(value, *others):
        held = {0: value}
        distances = [1 << k for k in range(1, n_row.bit_length() - 1)] + [1]
        for distance in distances:
            if distance == 1 and others:
                held = {d: after(v, *others) for d, v in held.items()}
            held |= {d ^ distance: exchange(v, "row", distance) for d, v in held.items()}
        return held

    corner, passed = over_planes(corner, None)
    rest, _ = over_planes(rest, passed)
    corner = over_row(corner)
    order = tuple(corner)
    device = index.reshape(1).astype(jnp.int32)
    work = begin_factor(device, order, list(corner.values()), side)
    rest = after(rest, work)
    work = go_on_factor(work)
    rest = over_row(rest, work)
    high, low, scales = end_factor(device, order, list(rest.values()), work, basis)
    first = jnp.where(core == 0, halves[0], halves[1])
    second = jnp.where(core == 0, halves[1], halves[0])
    products = jnp.concatenate([first, second], axis=1)
    new_basis = lax.dot_general(
        products, high, (((0,), (1,)), ((), ())), preferred_element_type=jnp.float32
    ) + lax.dot_general(products, low, (((0,), (1,)), ((), ())), preferred_element_type=jnp.float32)
    return (math.sqrt(ORDER) * new_basis, scales[0])


def solution(mesh):
    return jax.shard_map(
        local,
        mesh=mesh,
        in_specs=(P(("layers", "col"), "row"), P(("layers", "col"), "row")),
        out_specs=(P(("layers", "col"), "row"), P("layers")),
        check_vma=False,
    )
```
